32 devices in a mesh: col: 4 (over y, x), row: 8 (over z, core).
Axes of the slice: x: 2, y: 2, z: 4, core: 2. Of those that a mesh axis runs over, the one named last changes fastest.
Arguments:
- locked: float32 [1024, 131072], P('col', 'row'), may hold values from -6 to 6
- vectors: float32 [64, 131072], P(None, 'row'), may hold values from -125 to 125
- mass: float32 [131072], P('row'), may hold values from 0.18 to 3.5
Outputs:
- appended: float32 [64, 131072], P(None, 'row')
- factor: float32 [64, 64], replicated
The draws below stay inside these ranges and needn't reach their ends.
All inputs are finite; a program needn't handle non-finite values.
Results may differ from the reference program's by a relative error of at most 0.0003.
Values sent between devices are 32-bit elements; how exact they have to be, the bound alone decides.
No kernel may reach another device: no remote copies, remote signals or barrier semaphores. Data moves between devices by JAX's collectives and lax.ppermute only.
A program may use at most 128 MiB of HBM per device.

```python
import jax
import jax.numpy as jnp
from jax import lax

LOCKED = 1024
NEW = 64
NROWS = 131072


def locked_rows(key, count):
    base = jax.random.fold_in(key, 11)

    def one_row(index):
        sub = jax.random.fold_in(base, index)
        return jnp.clip(jax.random.normal(sub, (NROWS,), jnp.float32), -6.0, 6.0)
    return jax.vmap(one_row)(jnp.arange(count))


def draw_locked(key, part):
    return locked_rows(key, LOCKED)


def draw_vectors(key, part):
    shared = locked_rows(key, NEW)
    noise = jnp.clip(jax.random.normal(jax.random.fold_in(key, 12), (NEW, NROWS), jnp.float32), -6.0, 6.0)
    even = 0.6 * shared[0::2] + 0.8 * noise[0::2]
    odd = even + 0.007 * noise[1::2]
    base = jnp.stack([even, odd], axis=1).reshape(NEW, NROWS)
    colscale = 10.0 ** jax.random.uniform(jax.random.fold_in(key, 13), (NEW, 1), jnp.float32)
    return base * colscale


def draw_mass(key, part):
    position = jnp.arange(NROWS).astype(jnp.float32) / (NROWS - 1)
    rough = jnp.exp(jax.random.uniform(jax.random.fold_in(key, 15), (NROWS,), jnp.float32, -0.35, 0.35))
    rough = rough / 1.0204942
    trend = 0.5 + position
    return trend * rough


def setup_inputs(seed: int = 0) -> dict:
    key_of = jax.random.split(jax.random.key(seed), 4)
    locked = draw_locked(jax.random.fold_in(key_of[3], 71), 0)
    vectors = draw_vectors(jax.random.fold_in(key_of[3], 71), 0)
    mass = draw_mass(jax.random.fold_in(key_of[3], 71), 0)
    return dict(locked=locked, vectors=vectors, mass=mass)


def inner(left, right, mass):
    return jnp.dot(left * mass, right.T, precision=lax.Precision.HIGHEST) / NROWS

def factorize(gram):
    size = gram.shape[0]
    places = jnp.arange(size, dtype=jnp.int32)

    def step(index, state):
        work, lower = state
        column = lax.dynamic_slice_in_dim(work, index, 1, 1)[:, 0]
        pivot = jnp.sqrt(lax.dynamic_slice_in_dim(column, index, 1, 0)[0])
        column = jnp.where(places >= index, column / pivot, jnp.zeros_like(column))
        pick = (places == index).astype(work.dtype)
        lower = lower + column[:, None] * pick[None, :]
        work = work - column[:, None] * column[None, :]
        return (work, lower)
    work, lower = lax.fori_loop(0, size, step, (gram, jnp.zeros_like(gram)))
    return lower

def invert_lower(lower):
    size = lower.shape[0]
    places = jnp.arange(size, dtype=jnp.int32)

    def step(index, inverse):
        line = lax.dynamic_slice_in_dim(lower, index, 1, 0)[0]
        pick = (places == index).astype(lower.dtype)
        pivot = jnp.sum(line * pick)
        solved = (pick - jnp.dot(line, inverse, precision=lax.Precision.HIGHEST)) / pivot
        return inverse + pick[:, None] * solved[None, :]
    return lax.fori_loop(0, size, step, jnp.zeros_like(lower))

def project(block, locked, mass):
    coef = inner(locked, block, mass)
    return block - jnp.dot(coef.T, locked, precision=lax.Precision.HIGHEST)

def orthonormal(block, mass):
    gram = inner(block, block, mass)
    lower = factorize(gram)
    inverse = invert_lower(lower)
    return (jnp.dot(inverse, block, precision=lax.Precision.HIGHEST), lower.T)

def reference(locked, vectors, mass):
    once = project(vectors, locked, mass)
    projected = project(once, locked, mass)
    middle, upper_one = orthonormal(projected, mass)
    appended, upper_two = orthonormal(middle, mass)
    factor = jnp.dot(upper_two, upper_one, precision=lax.Precision.HIGHEST)
    return (appended, factor)
```

```python
import functools

import jax
import jax.numpy as jnp
from jax import lax
from jax.experimental import pallas as pl
from jax.experimental.pallas import tpu as pltpu
from jax.sharding import PartitionSpec as P

F32 = jnp.float32
BF16 = jnp.bfloat16
STEP = 512
VMEM_LIMIT = 48 * 1024 * 1024


def halves(x):
    high = x.astype(BF16)
    return high, (x - high.astype(F32)).astype(BF16)


def thirds(x):
    high = x.astype(BF16)
    rest = x - high.astype(F32)
    middle = rest.astype(BF16)
    return high, middle, (rest - middle.astype(F32)).astype(BF16)


def dot_nt(a, b):
    return lax.dot_general(a, b, (((1,), (1,)), ((), ())), preferred_element_type=F32)


def dot_nn(a, b):
    return lax.dot_general(a, b, (((1,), (0,)), ((), ())), preferred_element_type=F32)


def fold_rows(x, size):
    return (x[2 * size :] + x[size : 2 * size]) + x[:size]


def params():
    return pltpu.CompilerParams(vmem_limit_bytes=VMEM_LIMIT, dimension_semantics=("arbitrary",))


def cost(flops, nbytes):
    return pl.CostEstimate(flops=int(flops), bytes_accessed=int(nbytes), transcendentals=0)


def add_coefficients(acc_ref, locked_ref, block_ref, mass_ref):
    width = locked_ref.shape[1]
    for start in range(0, width, STEP):
        span = pl.ds(start, STEP)
        high, low = halves(locked_ref[:, span])
        pieces = jnp.concatenate(thirds(block_ref[:, span] * mass_ref[:, span]), axis=0)
        acc_ref[...] += dot_nt(
            jnp.concatenate([high, low], axis=1), jnp.concatenate([pieces, pieces], axis=1)
        )


def coefficients_kernel(separate, total, ids_ref, locked_ref, mass_ref, *refs):
    blocks, (out_ref, acc_ref) = refs[:-2], refs[-2:]
    step = pl.program_id(0)

    @pl.when(step == 0)
    def _():
        acc_ref[...] = jnp.zeros_like(acc_ref)

    if separate:
        for place, block_ref in enumerate(blocks):

            @pl.when(step == place)
            def _():
                add_coefficients(acc_ref, locked_ref, block_ref, mass_ref)
    else:
        add_coefficients(acc_ref, locked_ref, blocks[0], mass_ref)

    @pl.when(step == pl.num_programs(0) - 1)
    def _():
        out_ref[...] = fold_rows(acc_ref[...].T, out_ref.shape[0]) * (1.0 / total)


def coefficients(locked, mass, blocks, ids, unit, total):
    separate = isinstance(blocks, (list, tuple))
    held, steps = locked.shape[0], ids.shape[0]
    if not separate:
        blocks = [blocks]
    new = blocks[0].shape[0]
    block_spec = (
        pl.BlockSpec((new, unit), lambda i, ids: (0, 0))
        if separate
        else pl.BlockSpec((new, unit), lambda i, ids: (0, ids[i]))
    )
    return pl.pallas_call(
        functools.partial(coefficients_kernel, separate, total),
        out_shape=jax.ShapeDtypeStruct((new, held), F32),
        grid_spec=pltpu.PrefetchScalarGridSpec(
            num_scalar_prefetch=1,
            grid=(steps,),
            in_specs=[
                pl.BlockSpec((held, unit), lambda i, ids: (0, ids[i])),
                pl.BlockSpec((1, unit), lambda i, ids: (0, ids[i])),
            ]
            + [block_spec] * len(blocks),
            out_specs=pl.BlockSpec((new, held), lambda i, ids: (0, 0)),
            scratch_shapes=[pltpu.VMEM((held, 3 * new), F32)],
        ),
        compiler_params=params(),
        cost_estimate=cost(12 * held * new * steps * unit, 4 * (held + new) * steps * unit),
    )(ids, locked, mass, *blocks)


def corrections_kernel(count, base, extra, ids_ref, coef_ref, locked_ref, *refs):
    bases, refs = refs[: count if base == "list" else (1 if base else 0)], refs[count if base == "list" else (1 if base else 0) :]
    extras, outs = refs[: count * extra], refs[count * extra :]
    step = pl.program_id(0)
    size = coef_ref.shape[0]
    pieces = jnp.concatenate(thirds(coef_ref[...]), axis=0)
    pieces = jnp.concatenate([pieces, pieces], axis=1)
    for place in range(count):

        @pl.when(step == place)
        def _():
            for start in range(0, locked_ref.shape[1], STEP):
                span = pl.ds(start, STEP)
                high, low = halves(locked_ref[:, span])
                term = dot_nn(pieces, jnp.concatenate([high, low], axis=0))
                term = fold_rows(term, size)
                for one in range(extra):
                    term = term + extras[place * extra + one][:, span]
                if base:
                    term = bases[place if base == "list" else 0][:, span] - term
                outs[place][:, span] = term


def corrections(coef, locked, ids, unit, base=None, extras=()):
    held, count, new = locked.shape[0], ids.shape[0], coef.shape[0]
    extra = len(extras[0]) if extras else 0
    fixed = pl.BlockSpec((new, unit), lambda i, ids: (0, 0))
    flat = [x for group in extras for x in group]
    if base is None:
        kind, bases, base_specs = None, [], []
    elif isinstance(base, (list, tuple)):
        kind, bases, base_specs = "list", list(base), [fixed] * count
    else:
        kind, bases = "whole", [base]
        base_specs = [pl.BlockSpec((new, unit), lambda i, ids: (0, ids[i]))]
    return pl.pallas_call(
        functools.partial(corrections_kernel, count, kind, extra),
        out_shape=[jax.ShapeDtypeStruct((new, unit), F32)] * count,
        grid_spec=pltpu.PrefetchScalarGridSpec(
            num_scalar_prefetch=1,
            grid=(count,),
            in_specs=[
                pl.BlockSpec((new, held), lambda i, ids: (0, 0)),
                pl.BlockSpec((held, unit), lambda i, ids: (0, ids[i])),
            ]
            + base_specs
            + [fixed] * len(flat),
            out_specs=[fixed] * count,
        ),
        compiler_params=params(),
        cost_estimate=cost(12 * held * new * count * unit, 4 * (held + 2 * new) * count * unit),
    )(ids, coef, locked, *bases, *flat)


def eliminate(gram):
    size = gram.shape[0]
    rows = lax.broadcasted_iota(jnp.int32, (size, 2 * size), 0)
    lanes = lax.broadcasted_iota(jnp.int32, (size, 2 * size), 1)
    places = lax.broadcasted_iota(jnp.int32, (size, 1), 0)
    eye = (rows[:, :size] == lanes[:, :size]).astype(F32)
    work = jnp.concatenate([gram, eye], axis=1)
    scales = jnp.zeros((size, 1), F32)
    for index in range(size):
        line = work[index : index + 1, :]
        pivot = line[:, index : index + 1]
        scale = lax.rsqrt(pivot)
        scale = scale * (1.5 - 0.5 * pivot * scale * scale)
        line = line * scale
        column = jnp.where(places > index, work[:, index : index + 1] * scale, 0.0)
        scales = jnp.where(places == index, scale, scales)
        work = work - column * line
    work = work * scales
    upper = jnp.where(lanes >= rows, work, 0.0)[:, :size]
    return upper, work[:, size:]


def spread(matrix):
    pieces = jnp.concatenate(thirds(matrix), axis=0)
    return jnp.concatenate([pieces, pieces, pieces], axis=1)


def apply_left(spread_matrix, block):
    size = block.shape[0]
    return fold_rows(dot_nn(spread_matrix, jnp.concatenate(thirds(block), axis=0)), size)


def gram_of(block, mass):
    size = block.shape[0]
    left = jnp.concatenate(thirds(block * mass), axis=0)
    right = jnp.concatenate(thirds(block), axis=0)
    part = fold_rows(dot_nt(left, right), size)
    return (part[:, 2 * size :] + part[:, size : 2 * size]) + part[:, :size]


def own_gram_kernel(total, ids_ref, mass_ref, *refs):
    ins, outs = refs[:4], refs[4:]
    size = outs[0].shape[0]
    acc = jnp.zeros((size, size), F32)
    unit = outs[0].shape[1]
    for place in range(2):
        for start in range(0, unit, STEP):
            span = pl.ds(start, STEP)
            block = ins[place][:, span] - ins[2 + place][:, span]
            outs[place][:, span] = block
            where = pl.ds(pl.multiple_of(ids_ref[place] * unit + start, STEP), STEP)
            acc = acc + gram_of(block, mass_ref[:, where])
    outs[2][...] = acc * (1.0 / total)


def middle_kernel(total, ids_ref, mass_ref, gram_ref, a_ref, b_ref, gram_out, upper_out, inverse_out):
    upper, inverse = eliminate(gram_ref[...])
    upper_out[...] = upper
    inverse_out[...] = inverse
    left = spread(inverse)
    size, unit = a_ref.shape
    acc = jnp.zeros((size, size), F32)
    for place, block_ref in enumerate((a_ref, b_ref)):
        for start in range(0, unit, STEP):
            middle = apply_left(left, block_ref[:, pl.ds(start, STEP)])
            where = pl.ds(pl.multiple_of(ids_ref[place] * unit + start, STEP), STEP)
            acc = acc + gram_of(middle, mass_ref[:, where])
    gram_out[...] = acc * (1.0 / total)


def last_kernel(gram_ref, upper_ref, inverse_ref, factor_out, both_out):
    upper, inverse = eliminate(gram_ref[...])
    high = lax.Precision.HIGHEST
    factor_out[...] = jnp.dot(upper, upper_ref[...], precision=high, preferred_element_type=F32)
    both_out[...] = jnp.dot(inverse, inverse_ref[...], precision=high, preferred_element_type=F32)


def finish_kernel(count, ids_ref, both_ref, *refs):
    blocks, out_ref = refs[:-1], refs[-1]
    left = spread(both_ref[...])
    step = pl.program_id(0)
    for place in range(count):

        @pl.when(step == place)
        def _():
            for start in range(0, out_ref.shape[1], STEP):
                span = pl.ds(start, STEP)
                out_ref[:, span] = apply_left(left, blocks[place][:, span])


def flip(x, axis, bit):
    size = lax.axis_size(axis)
    return lax.ppermute(x, axis, [(i, i ^ bit) for i in range(size)])


def sum_over(x, axis):
    size = lax.axis_size(axis)
    bit = 1
    while bit < size:
        x = x + flip(x, axis, bit)
        bit *= 2
    return x


def local(locked, vectors, mass):
    new, rows = vectors.shape
    total = rows * lax.axis_size("row")
    unit = rows // 8
    mass = mass.reshape(1, rows)
    col = lax.axis_index("col")
    i, j = col % 2, col // 2
    k, m = 1 - i, 1 - j
    ids = lambda *xs: jnp.stack([jnp.asarray(x, jnp.int32) for x in xs])
    own = ids(2 * i + j, 4 + 2 * j + i)
    pass_on = ids(2 * i + m, 4 + 2 * j + k)
    away_first = ids(2 * k + m, 4 + 2 * m + k)
    away_second = ids(2 * k + j, 4 + 2 * m + i)

    def scatter_sum(coef, base):
        a1, b1 = corrections(coef, locked, away_first, unit)
        ra1, rb1 = flip(a1, "col", 1), flip(b1, "col", 2)
        a2, b2 = corrections(coef, locked, away_second, unit)
        ra2, rb2 = flip(a2, "col", 1), flip(b2, "col", 2)
        a3, b3 = corrections(coef, locked, pass_on, unit, extras=((ra1,), (rb1,)))
        ra3, rb3 = flip(a3, "col", 2), flip(b3, "col", 1)
        a4, b4 = corrections(coef, locked, own, unit, base=base, extras=((ra2,), (rb2,)))
        return (a4, b4), (ra3, rb3)

    def spread_out(a, b):
        ay, bx = flip(a, "col", 2), flip(b, "col", 1)
        ax, by = flip(a, "col", 1), flip(b, "col", 2)
        axy, bxy = flip(ay, "col", 1), flip(bx, "col", 2)
        return (ay, bx, ax, by), (axy, bxy)

    near = ids(2 * i + m, 4 + 2 * j + k, 2 * k + j, 4 + 2 * m + i)
    far = ids(2 * k + m, 4 + 2 * m + k)

    first = coefficients(locked, mass, vectors, jnp.arange(8, dtype=jnp.int32), unit, total)
    first = sum_over(first, "row")
    (a4, b4), (ra, rb) = scatter_sum(first, vectors)
    once = (a4 - ra, b4 - rb)
    near_units, far_units = spread_out(*once)
    second = coefficients(locked, mass, list(once), own, unit, total)
    second = second + coefficients(locked, mass, list(near_units), near, unit, total)
    second = second + coefficients(locked, mass, list(far_units), far, unit, total)
    second = sum_over(second, "row")
    (a4, b4), (ra, rb) = scatter_sum(second, list(once))

    square = jax.ShapeDtypeStruct((new, new), F32)
    smem = pl.BlockSpec(memory_space=pltpu.SMEM)
    vmem = pl.BlockSpec(memory_space=pltpu.VMEM)
    plain = pltpu.CompilerParams(vmem_limit_bytes=VMEM_LIMIT)
    a, b, gram = pl.pallas_call(
        functools.partial(own_gram_kernel, total),
        out_shape=[jax.ShapeDtypeStruct((new, unit), F32)] * 2 + [square],
        in_specs=[smem] + [vmem] * 5,
        out_specs=[vmem] * 3,
        compiler_params=plain,
        cost_estimate=cost(18 * new * new * 2 * unit, 24 * new * unit),
    )(own, mass, a4, b4, ra, rb)
    near_units, far_units = spread_out(a, b)
    gram = sum_over(sum_over(gram, "col"), "row")
    gram, upper, inverse = pl.pallas_call(
        functools.partial(middle_kernel, total),
        out_shape=[square] * 3,
        in_specs=[smem] + [vmem] * 4,
        out_specs=[vmem] * 3,
        compiler_params=plain,
        cost_estimate=cost(36 * new * new * 2 * unit, 8 * new * unit),
    )(own, mass, gram, a, b)
    gram = sum_over(sum_over(gram, "col"), "row")
    factor, both = pl.pallas_call(
        last_kernel,
        out_shape=[square] * 2,
        in_specs=[vmem] * 3,
        out_specs=[vmem] * 2,
        compiler_params=plain,
        cost_estimate=cost(1e6, 1e5),
    )(gram, upper, inverse)
    blocks = [a, b, *near_units, *far_units]
    appended = pl.pallas_call(
        functools.partial(finish_kernel, len(blocks)),
        out_shape=jax.ShapeDtypeStruct((new, rows), F32),
        grid_spec=pltpu.PrefetchScalarGridSpec(
            num_scalar_prefetch=1,
            grid=(len(blocks),),
            in_specs=[pl.BlockSpec((new, new), lambda i, ids: (0, 0))]
            + [pl.BlockSpec((new, unit), lambda i, ids: (0, 0))] * len(blocks),
            out_specs=pl.BlockSpec((new, unit), lambda i, ids: (0, ids[i])),
        ),
        compiler_params=params(),
        cost_estimate=cost(18 * new * new * rows, 8 * new * rows),
    )(jnp.concatenate([own, near, far]), both, *blocks)
    return (appended, factor)


def solution(mesh):
    return jax.shard_map(
        local,
        mesh=mesh,
        in_specs=(P("col", "row"), P(None, "row"), P("row")),
        out_specs=(P(None, "row"), P()),
        check_vma=False,
    )
```

```python
import functools

import jax
import jax.numpy as jnp
from jax import lax
from jax.experimental import pallas as pl
from jax.experimental.pallas import tpu as pltpu
from jax.sharding import PartitionSpec as P

F32 = jnp.float32
BF16 = jnp.bfloat16
STEP = 512
CHUNK = 1024
SLOTS = 4
VMEM_LIMIT = 30 * 1024 * 1024
FIRST_LIMIT = VMEM_LIMIT
SMEM = pl.BlockSpec(memory_space=pltpu.SMEM)
VMEM = pl.BlockSpec(memory_space=pltpu.VMEM)
HBM = pl.BlockSpec(memory_space=pltpu.HBM)
PARAMS = pltpu.CompilerParams(vmem_limit_bytes=VMEM_LIMIT)


def halves(x):
    high = x.astype(BF16)
    return high, (x - high.astype(F32)).astype(BF16)


def thirds(x):
    high = x.astype(BF16)
    rest = x - high.astype(F32)
    middle = rest.astype(BF16)
    low = (rest - middle.astype(F32)).astype(BF16)
    return jnp.concatenate([high, middle, low], axis=0)


def dot_nt(a, b):
    return lax.dot_general(a, b, (((1,), (1,)), ((), ())), preferred_element_type=F32)


def dot_nn(a, b):
    return lax.dot_general(a, b, (((1,), (0,)), ((), ())), preferred_element_type=F32)


def fold_rows(x, size):
    return (x[2 * size :] + x[size : 2 * size]) + x[:size]


def cost(flops, nbytes):
    return pl.CostEstimate(flops=int(flops), bytes_accessed=int(nbytes), transcendentals=0)


def array(*shape, dtype=F32):
    return jax.ShapeDtypeStruct(shape, dtype)


def columns(place, unit, start=0, width=None):
    return pl.ds(pl.multiple_of(place * unit + start, STEP), unit if width is None else width)


def first_kernel(total, locked, vectors, mass, out, high, low, mass_out, held_buf, new_buf, acc, sems, mass_sem):
    rows = locked.shape[1]
    count = rows // CHUNK

    def copies(index):
        span, slot = pl.ds(index * CHUNK, CHUNK), index % SLOTS
        return (
            pltpu.make_async_copy(vectors.at[:, span], new_buf.at[slot], sems.at[0, slot]),
            pltpu.make_async_copy(locked.at[:, span], held_buf.at[slot], sems.at[1, slot]),
        )

    mass_copy = pltpu.make_async_copy(mass, mass_out, mass_sem)
    mass_copy.start()
    for index in range(SLOTS - 1):
        for copy in copies(index):
            copy.start()
    mass_copy.wait()
    for index in range(count):
        if index + SLOTS - 1 < count:
            for copy in copies(index + SLOTS - 1):
                copy.start()
        for copy in copies(index):
            copy.wait()
        span, slot = pl.ds(index * CHUNK, CHUNK), index % SLOTS
        pieces = thirds(new_buf[slot] * mass_out[:, span])
        top, rest = halves(held_buf[slot])
        high[:, span] = top
        low[:, span] = rest
        term = dot_nt(jnp.concatenate([top, rest], axis=0), pieces)
        if index == 0:
            acc[...] = term
        else:
            acc[...] += term
    held = locked.shape[0]
    out[...] = fold_rows((acc[:held] + acc[held:]).T, out.shape[0]) * (1.0 / total)


def first_coefficients(locked, vectors, mass, total):
    (held, rows), new = locked.shape, vectors.shape[0]
    return pl.pallas_call(
        functools.partial(first_kernel, total),
        out_shape=[
            array(new, held),
            array(held, rows, dtype=BF16),
            array(held, rows, dtype=BF16),
            array(1, rows),
        ],
        in_specs=[HBM] * 3,
        out_specs=[VMEM] * 4,
        scratch_shapes=[
            pltpu.VMEM((SLOTS, held, CHUNK), F32),
            pltpu.VMEM((SLOTS, new, CHUNK), F32),
            pltpu.VMEM((2 * held, 3 * new), F32),
            pltpu.SemaphoreType.DMA((2, SLOTS)),
            pltpu.SemaphoreType.DMA,
        ],
        compiler_params=pltpu.CompilerParams(vmem_limit_bytes=FIRST_LIMIT),
        cost_estimate=cost(12 * held * new * rows, 8 * held * rows),
    )(locked, vectors, mass)


def fold_gram(x, size):
    part = fold_rows(x, size)
    return (part[:, 2 * size :] + part[:, size : 2 * size]) + part[:, :size]


def second_kernel(count, total, mode, ids, high, low, mass, *refs):
    blocks, rest = refs[:count], refs[count:]
    new, unit = blocks[0].shape
    held = high.shape[0]
    if mode == "own":
        out, grams, acc = rest
    elif mode == "near":
        base, out, grams, acc = rest
    else:
        base, own_grams, near_grams, out, acc, grams = rest
    for place in range(count):
        span = columns(ids[place], unit)
        block = blocks[place][...]
        pieces = thirds(block * mass[:, span])
        left = jnp.concatenate([high[:, span], low[:, span], thirds(block)], axis=0)
        term = dot_nt(left, pieces)
        grams[ids[place] if mode == "far" else place] = fold_gram(term[2 * held :], new)
        if place == 0:
            acc[...] = term[: 2 * held]
        else:
            acc[...] += term[: 2 * held]
    second = fold_rows((acc[:held] + acc[held:]).T, new)
    if mode != "own":
        second = second + base[...]
    if mode != "far":
        out[...] = second
        return
    for place in range(2):
        grams[ids[2 + place]] = own_grams[place]
    for place in range(4):
        grams[ids[4 + place]] = near_grams[place]
    gram = grams[0]
    for place in range(1, 8):
        gram = gram + grams[place]
    out[...] = jnp.concatenate([second, gram, jnp.zeros_like(gram)], axis=1) * (1.0 / total)


def second_coefficients(mode, ids, high, low, mass, blocks, total, *others):
    new, unit = blocks[0].shape
    held, count = high.shape[0], len(blocks)
    scratch = [pltpu.VMEM((2 * held, 3 * new), F32)]
    if mode == "far":
        shapes = [array(new, held + 2 * new)]
        scratch.append(pltpu.VMEM((8, new, new), F32))
    else:
        shapes = [array(new, held), array(count, new, new)]
    return pl.pallas_call(
        functools.partial(second_kernel, count, total, mode),
        out_shape=shapes,
        in_specs=[SMEM] + [VMEM] * (3 + count + len(others)),
        out_specs=[VMEM] * len(shapes),
        scratch_shapes=scratch,
        compiler_params=PARAMS,
        cost_estimate=cost(14 * held * new * count * unit, 4 * (held + new) * count * unit),
    )(ids, high, low, mass, *blocks, *others)


def corrections_kernel(count, ids, coef, high, low, *outs):
    new, unit = outs[0].shape
    held = high.shape[0]
    pieces = thirds(coef[:, :held])
    pieces = jnp.concatenate([pieces, pieces], axis=1)
    for place in range(count):
        for start in range(0, unit, STEP):
            span = columns(ids[place], unit, start, STEP)
            term = dot_nn(pieces, jnp.concatenate([high[:, span], low[:, span]], axis=0))
            outs[place][:, pl.ds(start, STEP)] = fold_rows(term, new)


def corrections(ids, coef, high, low, unit):
    new, held, count = coef.shape[0], high.shape[0], ids.shape[0]
    return pl.pallas_call(
        functools.partial(corrections_kernel, count),
        out_shape=[array(new, unit)] * count,
        in_specs=[SMEM] + [VMEM] * 3,
        out_specs=[VMEM] * count,
        compiler_params=PARAMS,
        cost_estimate=cost(12 * held * new * count * unit, 4 * (held + new) * count * unit),
    )(ids, coef, high, low)


def eliminate(gram):
    size = gram.shape[0]
    rows = lax.broadcasted_iota(jnp.int32, (size, 2 * size), 0)
    lanes = lax.broadcasted_iota(jnp.int32, (size, 2 * size), 1)
    places = lax.broadcasted_iota(jnp.int32, (size, 1), 0)
    eye = (rows[:, :size] == lanes[:, :size]).astype(F32)
    work = jnp.concatenate([gram, eye], axis=1)
    scales = jnp.zeros((size, 1), F32)
    for index in range(size):
        line = work[index : index + 1, :]
        pivot = line[:, index : index + 1]
        scale = lax.rsqrt(pivot)
        scale = scale * (1.5 - 0.5 * pivot * scale * scale)
        line = line * scale
        column = jnp.where(places > index, work[:, index : index + 1] * scale, 0.0)
        scales = jnp.where(places == index, scale, scales)
        work = work - column * line
    work = work * scales
    upper = jnp.where(lanes >= rows, work, 0.0)[:, :size]
    return upper, work[:, size:]


def spread(matrix):
    pieces = thirds(matrix)
    return jnp.concatenate([pieces, pieces, pieces], axis=1)


def apply_left(spread_matrix, block):
    return fold_rows(dot_nn(spread_matrix, thirds(block)), block.shape[0])


def gram_of(block, mass):
    size = block.shape[0]
    return fold_gram(dot_nt(thirds(block * mass), thirds(block)), size)


def factor_kernel(both, upper_out, inverse_out):
    size = upper_out.shape[0]
    held = both.shape[1] - 2 * size
    upper_out[...], inverse_out[...] = eliminate(both[:, held : held + size])


def middle_kernel(total, ids, mass, inverse, *refs):
    ins, outs = refs[:4], refs[4:]
    new, unit = outs[0].shape
    left = spread(inverse[...])
    acc = jnp.zeros((new, new), F32)
    for place in range(2):
        for start in range(0, unit, STEP):
            span = pl.ds(start, STEP)
            middle = apply_left(left, ins[place][:, span] - ins[2 + place][:, span])
            outs[place][:, span] = middle
            acc = acc + gram_of(middle, mass[:, columns(ids[place], unit, start, STEP)])
    outs[2][...] = acc * (1.0 / total)


def last_kernel(gram, upper_one, factor_out, inverse_out):
    upper, inverse = eliminate(gram[...])
    factor_out[...] = jnp.dot(
        upper, upper_one[...], precision=lax.Precision.HIGHEST, preferred_element_type=F32
    )
    inverse_out[...] = inverse


def finish_kernel(count, ids, inverse, *refs):
    blocks, out = refs[:count], refs[-1]
    left = spread(inverse[...])
    step = pl.program_id(0)
    for place in range(count):

        @pl.when(step == place)
        def _():
            for start in range(0, out.shape[1], STEP):
                span = pl.ds(start, STEP)
                out[:, span] = apply_left(left, blocks[place][:, span])


def finish(ids, inverse, blocks, rows, target=None):
    new, unit = blocks[0].shape
    count = len(blocks)
    extra = [] if target is None else [target]
    whole = lambda shape: pl.BlockSpec(shape, lambda i, ids: (0, 0))
    return pl.pallas_call(
        functools.partial(finish_kernel, count),
        out_shape=array(new, rows),
        grid_spec=pltpu.PrefetchScalarGridSpec(
            num_scalar_prefetch=1,
            grid=(count,),
            in_specs=[whole((new, new))]
            + [whole((new, unit))] * count
            + [pl.BlockSpec(memory_space=pl.ANY)] * len(extra),
            out_specs=pl.BlockSpec((new, unit), lambda i, ids: (0, ids[i])),
        ),
        input_output_aliases={} if target is None else {2 + count: 0},
        compiler_params=PARAMS,
        cost_estimate=cost(18 * new * new * count * unit, 8 * new * count * unit),
    )(ids, inverse, *blocks, *extra)


def flip(x, axis, bit):
    size = lax.axis_size(axis)
    return lax.ppermute(x, axis, [(i, i ^ bit) for i in range(size)])


def sum_over(x, axis):
    size = lax.axis_size(axis)
    bit = 1
    while bit < size:
        x = x + flip(x, axis, bit)
        bit *= 2
    return x


def sum_of_four(x, axis):
    one, two, three = flip(x, axis, 1), flip(x, axis, 2), flip(x, axis, 3)
    return (x + one) + (two + three)


def local(locked, vectors, mass):
    new, rows = vectors.shape
    total = rows * lax.axis_size("row")
    unit = rows // 8
    col = lax.axis_index("col")
    i, j = col % 2, col // 2
    k, m = 1 - i, 1 - j
    ids = lambda *xs: jnp.stack([jnp.asarray(x, jnp.int32) for x in xs])
    own = (2 * i + j, 4 + 2 * j + i)
    pass_on = (2 * i + m, 4 + 2 * j + k)
    away_first = (2 * k + m, 4 + 2 * m + k)
    away_second = (2 * k + j, 4 + 2 * m + i)
    near = ids(*pass_on, *away_second)
    far = ids(*away_first)

    first, high, low, mass = first_coefficients(locked, vectors, mass.reshape(1, rows), total)

    def scatter_sum(coef, base):
        a1, b1 = corrections(ids(*away_first), coef, high, low, unit)
        ra1, rb1 = flip(a1, "col", 1), flip(b1, "col", 2)
        a2, b2 = corrections(ids(*away_second), coef, high, low, unit)
        ra2, rb2 = flip(a2, "col", 1), flip(b2, "col", 2)
        a3, b3, a4, b4 = corrections(ids(*pass_on, *own), coef, high, low, unit)
        ra3, rb3 = flip(a3 + ra1, "col", 2), flip(b3 + rb1, "col", 1)
        return (base[0] - (a4 + ra2), base[1] - (b4 + rb2)), (ra3, rb3)

    def spread_out(a, b):
        ay, bx = flip(a, "col", 2), flip(b, "col", 1)
        ax, by = flip(a, "col", 1), flip(b, "col", 2)
        return (ay, bx, ax, by), (flip(ay, "col", 1), flip(bx, "col", 2))

    first = sum_over(first, "row")
    here = [lax.dynamic_slice_in_dim(vectors, place * unit, unit, 1) for place in own]
    (a, b), (ra, rb) = scatter_sum(first, here)
    once = (a - ra, b - rb)
    near_units, far_units = spread_out(*once)
    order = jnp.concatenate([far, ids(*own), near])
    second, grams = second_coefficients("own", ids(*own), high, low, mass, once, total)
    second, more = second_coefficients("near", near, high, low, mass, near_units, total, second)
    (second,) = second_coefficients("far", order, high, low, mass, far_units, total, second, grams, more)
    second = sum_over(second, "row")
    (a, b), (ra, rb) = scatter_sum(second, once)

    upper, inverse = pl.pallas_call(
        factor_kernel,
        out_shape=[array(new, new)] * 2,
        in_specs=[VMEM],
        out_specs=[VMEM] * 2,
        compiler_params=PARAMS,
        cost_estimate=cost(1e6, 1e5),
    )(second)
    a, b, gram = pl.pallas_call(
        functools.partial(middle_kernel, total),
        out_shape=[array(new, unit)] * 2 + [array(new, new)],
        in_specs=[SMEM] + [VMEM] * 6,
        out_specs=[VMEM] * 3,
        compiler_params=PARAMS,
        cost_estimate=cost(36 * new * new * 2 * unit, 24 * new * unit),
    )(ids(*own), mass, inverse, a, b, ra, rb)
    ay, bx = flip(a, "col", 2), flip(b, "col", 1)
    gram = sum_of_four(gram, "col")
    gram, late_a, late_b, ay, bx = lax.optimization_barrier((gram, a, b, ay, bx))
    ax, by = flip(late_a, "col", 1), flip(late_b, "col", 2)
    near_units, far_units = (ay, bx, ax, by), (flip(ay, "col", 1), flip(bx, "col", 2))
    gram = sum_over(gram, "row")
    factor, inverse = pl.pallas_call(
        last_kernel,
        out_shape=[array(new, new)] * 2,
        in_specs=[VMEM] * 2,
        out_specs=[VMEM] * 2,
        compiler_params=PARAMS,
        cost_estimate=cost(1e6, 1e5),
    )(gram, upper)
    appended = finish(jnp.concatenate([ids(*own), near]), inverse, (a, b, *near_units), rows)
    appended = finish(far, inverse, far_units, rows, appended)
    return (appended, factor)


def solution(mesh):
    return jax.shard_map(
        local,
        mesh=mesh,
        in_specs=(P("col", "row"), P(None, "row"), P("row")),
        out_specs=(P(None, "row"), P()),
        check_vma=False,
    )
```

```python
import functools

import jax
import jax.numpy as jnp
from jax import lax
from jax.experimental import pallas as pl
from jax.experimental.pallas import tpu as pltpu
from jax.sharding import PartitionSpec as P

F32 = jnp.float32
BF16 = jnp.bfloat16
STEP = 1024
CHUNK = 1024
SLOTS = 4
ROWS = 16
GROUP = 4
VMEM_LIMIT = 24 * 1024 * 1024
VMEM = pl.BlockSpec(memory_space=pltpu.VMEM)
HBM = pl.BlockSpec(memory_space=pltpu.HBM)
NEAR, FAR = ("pass_on", "away_second"), ("away_first",)
PARAMS = pltpu.CompilerParams(vmem_limit_bytes=VMEM_LIMIT)


def halves(x):
    high = x.astype(BF16)
    return high, (x - high.astype(F32)).astype(BF16)


def thirds(x):
    high = x.astype(BF16)
    rest = x - high.astype(F32)
    middle = rest.astype(BF16)
    low = (rest - middle.astype(F32)).astype(BF16)
    return jnp.concatenate([high, middle, low], axis=0)


def put_halves(high, low, span, source):
    for row in range(0, source.shape[0], ROWS):
        here = pl.ds(row, ROWS)
        high[here, span], low[here, span] = halves(source[here, :])


def put_thirds(target, source, weights=None):
    size = source.shape[0]
    for row in range(0, size, ROWS):
        part = source[pl.ds(row, ROWS), :]
        part = thirds(part if weights is None else part * weights)
        for third in range(3):
            target[pl.ds(third * size + row, ROWS), :] = part[third * ROWS : (third + 1) * ROWS]


def dot_nt(a, b):
    return lax.dot_general(a, b, (((1,), (1,)), ((), ())), preferred_element_type=F32)


def dot_nn(a, b):
    return lax.dot_general(a, b, (((1,), (0,)), ((), ())), preferred_element_type=F32)


def fold_rows(x, size):
    return (x[2 * size :] + x[size : 2 * size]) + x[:size]


def cost(flops, nbytes):
    return pl.CostEstimate(flops=int(flops), bytes_accessed=int(nbytes), transcendentals=0)


def array(*shape, dtype=F32):
    return jax.ShapeDtypeStruct(shape, dtype)


def columns(place, unit, start=0, width=None):
    return pl.ds(pl.multiple_of(place * unit + start, STEP), unit if width is None else width)


def unit_places():
    col = lax.axis_index("col")
    i, j = lax.rem(col, 2), lax.div(col, 2)
    k, m = 1 - i, 1 - j
    return {
        "own": (2 * i + j, 4 + 2 * j + i),
        "pass_on": (2 * i + m, 4 + 2 * j + k),
        "away_first": (2 * k + m, 4 + 2 * m + k),
        "away_second": (2 * k + j, 4 + 2 * m + i),
    }


def places_of(*names):
    places = unit_places()
    return [place for name in names for place in places[name]]


def first_kernel(
    total, locked, vectors, mass, out, high, low, mass_out, here_a, here_b, held_buf, new_buf, pieces, acc, sems, more_sems
):
    held, rows = locked.shape
    unit = here_a.shape[1]
    count = rows // CHUNK

    def copies(index):
        span, slot = pl.ds(index * CHUNK, CHUNK), index % SLOTS
        return (
            pltpu.make_async_copy(vectors.at[:, span], new_buf.at[slot], sems.at[0, slot]),
            pltpu.make_async_copy(locked.at[:, span], held_buf.at[slot], sems.at[1, slot]),
        )

    mass_copy = pltpu.make_async_copy(mass, mass_out, more_sems.at[0])
    mass_copy.start()
    for index in range(SLOTS - 1):
        for copy in copies(index):
            copy.start()
    places = places_of("own")
    own_copies = [
        pltpu.make_async_copy(vectors.at[:, columns(place, unit)], here, more_sems.at[1 + which])
        for which, (place, here) in enumerate(zip(places, (here_a, here_b)))
    ]
    mass_copy.wait()
    for index in range(count + 1):
        if index < count:
            if index + SLOTS - 1 < count:
                for copy in copies(index + SLOTS - 1):
                    copy.start()
            if index == count // 2:
                for copy in own_copies:
                    copy.start()
            for copy in copies(index):
                copy.wait()
        if index > 0:
            span = pl.ds((index - 1) * CHUNK, CHUNK)
            left = jnp.concatenate([high[:, span], low[:, span]], axis=0)
            term = dot_nt(left, pieces[(index - 1) % 2])
            if index == 1:
                acc[...] = term
            else:
                acc[...] += term
        if index < count:
            span, slot = pl.ds(index * CHUNK, CHUNK), index % SLOTS
            put_thirds(pieces.at[index % 2], new_buf.at[slot], mass_out[:, span])
            put_halves(high, low, span, held_buf.at[slot])
    for copy in own_copies:
        copy.wait()
    out[...] = fold_rows((acc[:held] + acc[held:]).T, out.shape[0]) * (1.0 / total)


def first_coefficients(locked, vectors, mass, unit, total):
    (held, rows), new = locked.shape, vectors.shape[0]
    in_hbm = [pltpu.with_memory_space_constraint(x, pltpu.HBM) for x in (locked, vectors, mass)]
    return pl.pallas_call(
        functools.partial(first_kernel, total),
        out_shape=[
            array(new, held),
            array(held, rows, dtype=BF16),
            array(held, rows, dtype=BF16),
            array(1, rows),
            array(new, unit),
            array(new, unit),
        ],
        in_specs=[HBM] * 3,
        out_specs=[VMEM] * 6,
        scratch_shapes=[
            pltpu.VMEM((SLOTS, held, CHUNK), F32),
            pltpu.VMEM((SLOTS, new, CHUNK), F32),
            pltpu.VMEM((2, 3 * new, CHUNK), BF16),
            pltpu.VMEM((2 * held, 3 * new), F32),
            pltpu.SemaphoreType.DMA((2, SLOTS)),
            pltpu.SemaphoreType.DMA((3,)),
        ],
        compiler_params=PARAMS,
        cost_estimate=cost(12 * held * new * rows, 8 * held * rows),
    )(*in_hbm)


def fold_gram(x, size):
    part = fold_rows(x, size)
    return (part[:, 2 * size :] + part[:, size : 2 * size]) + part[:, :size]


def second_kernel(count, total, mode, high, low, mass, *refs):
    blocks, rest = refs[:count], refs[count:]
    new, unit = blocks[0].shape
    held = high.shape[0]
    rest, (acc, plain, weighted) = rest[:-3], rest[-3:]
    if mode == "own":
        out, grams = rest
    elif mode == "near":
        base, out, grams = rest
    else:
        base, own_grams, near_grams, out, grams = rest
    parts = {"own": ("own",), "near": NEAR, "far": FAR + ("own",) + NEAR}[mode]
    ids = places_of(*parts)
    for place in range(count):
        span = columns(ids[place], unit)
        put_thirds(weighted.at[place], blocks[place], mass[:, span])
        put_thirds(plain.at[place], blocks[place])
        left = jnp.concatenate([high[:, span], low[:, span], plain[place]], axis=0)
        term = dot_nt(left, weighted[place])
        grams[ids[place] if mode == "far" else place] = fold_gram(term[2 * held :], new)
        if place == 0:
            acc[...] = term[: 2 * held]
        else:
            acc[...] += term[: 2 * held]
    second = fold_rows((acc[:held] + acc[held:]).T, new)
    if mode != "own":
        second = second + base[...]
    if mode != "far":
        out[...] = second
        return
    for place in range(2):
        grams[ids[2 + place]] = own_grams[place]
    for place in range(4):
        grams[ids[4 + place]] = near_grams[place]
    gram = grams[0]
    for place in range(1, 8):
        gram = gram + grams[place]
    out[...] = jnp.concatenate([second, gram, jnp.zeros_like(gram)], axis=1) * (1.0 / total)


def second_coefficients(mode, high, low, mass, blocks, total, *others):
    new, unit = blocks[0].shape
    held, count = high.shape[0], len(blocks)
    pieces = pltpu.VMEM((count, 3 * new, unit), BF16)
    scratch = [pltpu.VMEM((2 * held, 3 * new), F32), pieces, pieces]
    if mode == "far":
        shapes = [array(new, held + 2 * new)]
        scratch.insert(0, pltpu.VMEM((8, new, new), F32))
    else:
        shapes = [array(new, held), array(count, new, new)]
    return pl.pallas_call(
        functools.partial(second_kernel, count, total, mode),
        out_shape=shapes,
        in_specs=[VMEM] * (3 + count + len(others)),
        out_specs=[VMEM] * len(shapes),
        scratch_shapes=scratch,
        compiler_params=PARAMS,
        cost_estimate=cost(14 * held * new * count * unit, 4 * (held + new) * count * unit),
    )(high, low, mass, *blocks, *others)


def corrections_kernel(names, bases, coef, high, low, *refs):
    base, outs = refs[:bases], refs[bases:]
    new, unit = outs[0].shape
    held = high.shape[0]
    pieces = thirds(coef[:, :held])
    pieces = jnp.concatenate([pieces, pieces], axis=1)
    places = places_of(*names)
    for which, place in enumerate(places):
        taken_off = which - (len(places) - bases)
        for start in range(0, unit, STEP):
            span, here = columns(place, unit, start, STEP), pl.ds(start, STEP)
            term = dot_nn(pieces, jnp.concatenate([high[:, span], low[:, span]], axis=0))
            term = fold_rows(term, new)
            outs[which][:, here] = base[taken_off][:, here] - term if taken_off >= 0 else term


def corrections(names, coef, high, low, unit, base=()):
    new, held, count = coef.shape[0], high.shape[0], 2 * len(names)
    return pl.pallas_call(
        functools.partial(corrections_kernel, names, len(base)),
        out_shape=[array(new, unit)] * count,
        in_specs=[VMEM] * (3 + len(base)),
        out_specs=[VMEM] * count,
        compiler_params=PARAMS,
        cost_estimate=cost(12 * held * new * count * unit, 4 * (held + new) * count * unit),
    )(coef, high, low, *base)


def take_off_kernel(*refs):
    for place in range(2):
        refs[6 + place][...] = refs[place][...] - refs[2 + place][...] - refs[4 + place][...]


def eliminate(gram):
    size = gram.shape[0]
    shape = (size, 2 * size)
    rows = lax.broadcasted_iota(jnp.int32, shape, 0)
    lanes = lax.broadcasted_iota(jnp.int32, shape, 1)
    eye = (rows[:, :size] == lanes[:, :size]).astype(F32)
    work = jnp.concatenate([gram, eye], axis=1)
    for start in range(0, size, GROUP):
        group = range(start, start + GROUP)
        column = {k: jnp.broadcast_to(work[:, k : k + 1], shape) for k in group}
        line = {k: work[k : k + 1, :] for k in group}
        for k in group:
            inverse = 1.0 / column[k][k : k + 1, :]
            scaled = line[k] * inverse
            for later in range(k + 1, start + GROUP):
                line[later] = line[later] - column[k][later : later + 1, :] * scaled
                column[later] = column[later] - column[k] * (column[later][k : k + 1, :] * inverse)
            work = work - jnp.where(rows > k, column[k], 0.0) * scaled
    pivots = jnp.sum(jnp.where(lanes == rows, work, 0.0), axis=1, keepdims=True)
    scale = lax.rsqrt(pivots)
    work = work * (scale * (1.5 - 0.5 * pivots * scale * scale))
    upper = jnp.where(lanes >= rows, work, 0.0)[:, :size]
    return upper, work[:, size:]


def spread(matrix):
    pieces = thirds(matrix)
    return jnp.concatenate([pieces, pieces, pieces], axis=1)


def apply_left(spread_matrix, block):
    return fold_rows(dot_nn(spread_matrix, thirds(block)), block.shape[0])


def gram_of(block, mass):
    size = block.shape[0]
    return fold_gram(dot_nt(thirds(block * mass), thirds(block)), size)


def factor_kernel(both, upper_out, inverse_out):
    size = upper_out.shape[0]
    held = both.shape[1] - 2 * size
    upper_out[...], inverse_out[...] = eliminate(both[:, held : held + size])


def middle_kernel(total, mass, inverse, *refs):
    ins, outs = refs[:6], refs[6:]
    new, unit = outs[0].shape
    left = spread(inverse[...])
    places = places_of("own")
    acc = jnp.zeros((new, new), F32)
    for which, place in enumerate(places):
        for start in range(0, unit, STEP):
            span = pl.ds(start, STEP)
            projected = ins[which][:, span] - ins[2 + which][:, span] - ins[4 + which][:, span]
            middle = apply_left(left, projected)
            outs[which][:, span] = middle
            acc = acc + gram_of(middle, mass[:, columns(place, unit, start, STEP)])
    outs[2][...] = acc * (1.0 / total)


def last_kernel(gram, upper_one, factor_out, inverse_out):
    upper, inverse = eliminate(gram[...])
    factor_out[...] = jnp.dot(
        upper, upper_one[...], precision=lax.Precision.HIGHEST, preferred_element_type=F32
    )
    inverse_out[...] = inverse


def finish_kernel(names, inverse, *refs):
    count = 2 * len(names)
    blocks, (out, buf, sems) = refs[:count], refs[-3:]
    unit = blocks[0].shape[1]
    left = spread(inverse[...])
    copies = []
    for which, place in enumerate(places_of(*names)):
        for start in range(0, unit, STEP):
            span = pl.ds(start, STEP)
            buf[which, :, span] = apply_left(left, blocks[which][:, span])
        copy = pltpu.make_async_copy(buf.at[which], out.at[:, columns(place, unit)], sems.at[which])
        copy.start()
        copies.append(copy)
    for copy in copies:
        copy.wait()


def finish(names, inverse, blocks, rows, target=None):
    new, unit = blocks[0].shape
    count = len(blocks)
    extra = [] if target is None else [target]
    return pl.pallas_call(
        functools.partial(finish_kernel, names),
        out_shape=array(new, rows),
        in_specs=[VMEM] * (1 + count) + [HBM] * len(extra),
        out_specs=HBM,
        scratch_shapes=[pltpu.VMEM((count, new, unit), F32), pltpu.SemaphoreType.DMA((count,))],
        input_output_aliases={} if target is None else {1 + count: 0},
        compiler_params=PARAMS,
        cost_estimate=cost(18 * new * new * count * unit, 8 * new * count * unit),
    )(inverse, *blocks, *extra)


def flip(x, axis, bit):
    size = lax.axis_size(axis)
    return lax.ppermute(x, axis, [(i, i ^ bit) for i in range(size)])


def sum_over(x, axis):
    size = lax.axis_size(axis)
    bit = 1
    while bit < size:
        x = x + flip(x, axis, bit)
        bit *= 2
    return x


def sum_of_four(x, axis, bit=1):
    one, two, three = (flip(x, axis, n * bit) for n in (1, 2, 3))
    return (x + one) + (two + three)


def sum_by_fours(x, axis):
    size = lax.axis_size(axis)
    x = x + flip(x, axis, 1)
    bit = 2
    while bit < size:
        if 2 * bit < size:
            x = sum_of_four(x, axis, bit)
        else:
            x = x + flip(x, axis, bit)
        bit *= 4
    return x


def local(locked, vectors, mass):
    new, rows = vectors.shape
    total = rows * lax.axis_size("row")
    unit = rows // 8
    first, high, low, mass, *here = first_coefficients(locked, vectors, mass.reshape(1, rows), unit, total)

    def scatter_sum(coef, base):
        a1, b1 = corrections(("away_first",), coef, high, low, unit)
        ra1, rb1 = flip(a1, "col", 1), flip(b1, "col", 2)
        a2, b2 = corrections(("away_second",), coef, high, low, unit)
        ra2, rb2 = flip(a2, "col", 1), flip(b2, "col", 2)
        a3, b3, a4, b4 = corrections(("pass_on", "own"), coef, high, low, unit, base)
        ra3, rb3 = flip(a3 + ra1, "col", 2), flip(b3 + rb1, "col", 1)
        return a4, b4, ra2, rb2, ra3, rb3

    first = sum_over(first, "row")
    once = pl.pallas_call(
        take_off_kernel,
        out_shape=[array(new, unit)] * 2,
        in_specs=[VMEM] * 6,
        out_specs=[VMEM] * 2,
        compiler_params=PARAMS,
        cost_estimate=cost(6 * new * unit, 32 * new * unit),
    )(*scatter_sum(first, here))
    a, b = once
    ay, bx = flip(a, "col", 2), flip(b, "col", 1)
    ax, by = flip(a, "col", 1), flip(b, "col", 2)
    far = flip(ay, "col", 1), flip(bx, "col", 2)
    second, grams = second_coefficients("own", high, low, mass, once, total)
    second, more = second_coefficients("near", high, low, mass, (ay, bx, ax, by), total, second)
    (second,) = second_coefficients("far", high, low, mass, far, total, second, grams, more)
    second = sum_over(second, "row")
    parts = scatter_sum(second, once)

    upper, inverse = pl.pallas_call(
        factor_kernel,
        out_shape=[array(new, new)] * 2,
        in_specs=[VMEM],
        out_specs=[VMEM] * 2,
        compiler_params=PARAMS,
        cost_estimate=cost(1e6, 1e5),
    )(second)
    a, b, gram = pl.pallas_call(
        functools.partial(middle_kernel, total),
        out_shape=[array(new, unit)] * 2 + [array(new, new)],
        in_specs=[VMEM] * 8,
        out_specs=[VMEM] * 3,
        compiler_params=PARAMS,
        cost_estimate=cost(36 * new * new * 2 * unit, 24 * new * unit),
    )(mass, inverse, *parts)
    ay, bx = flip(a, "col", 2), flip(b, "col", 1)
    ax, by = flip(a, "col", 1), flip(b, "col", 2)
    gram = sum_of_four(sum_by_fours(gram, "row"), "col")
    gram, ay, bx = lax.optimization_barrier((gram, ay, bx))
    far = flip(ay, "col", 1), flip(bx, "col", 2)
    factor, inverse = pl.pallas_call(
        last_kernel,
        out_shape=[array(new, new)] * 2,
        in_specs=[VMEM] * 2,
        out_specs=[VMEM] * 2,
        compiler_params=PARAMS,
        cost_estimate=cost(5e9, 1e5),
    )(gram, upper)
    appended = finish(("own",) + NEAR, inverse, (a, b, ay, bx, ax, by), rows)
    appended = finish(FAR, inverse, far, rows, appended)
    return (appended, factor)


def solution(mesh):
    return jax.shard_map(
        local,
        mesh=mesh,
        in_specs=(P("col", "row"), P(None, "row"), P("row")),
        out_specs=(P(None, "row"), P()),
        check_vma=False,
    )
```

```python
import functools

import jax
import jax.numpy as jnp
from jax import lax
from jax.experimental import pallas as pl
from jax.experimental.pallas import tpu as pltpu
from jax.sharding import PartitionSpec as P

F32 = jnp.float32
BF16 = jnp.bfloat16
STEP = 1024
CHUNK = 2048
SLOTS = 4
ROWS = 16
GROUP = 4
VMEM_LIMIT = 24 * 1024 * 1024
VMEM = pl.BlockSpec(memory_space=pltpu.VMEM)
HBM = pl.BlockSpec(memory_space=pltpu.HBM)
NEAR, FAR = ("pass_on", "away_second"), ("away_first",)
PARAMS = pltpu.CompilerParams(vmem_limit_bytes=VMEM_LIMIT)


def halves(x):
    high = x.astype(BF16)
    return high, (x - high.astype(F32)).astype(BF16)


def thirds(x):
    high = x.astype(BF16)
    rest = x - high.astype(F32)
    middle = rest.astype(BF16)
    low = (rest - middle.astype(F32)).astype(BF16)
    return jnp.concatenate([high, middle, low], axis=0)


def put_halves(high, low, span, source):
    for row in range(0, source.shape[0], ROWS):
        here = pl.ds(row, ROWS)
        high[here, span], low[here, span] = halves(source[here, :])


def put_thirds(target, source, weights=None):
    size = source.shape[0]
    for row in range(0, size, ROWS):
        part = source[pl.ds(row, ROWS), :]
        part = thirds(part if weights is None else part * weights)
        for third in range(3):
            target[pl.ds(third * size + row, ROWS), :] = part[third * ROWS : (third + 1) * ROWS]


def dot_nt(a, b):
    return lax.dot_general(a, b, (((1,), (1,)), ((), ())), preferred_element_type=F32)


def dot_nn(a, b):
    return lax.dot_general(a, b, (((1,), (0,)), ((), ())), preferred_element_type=F32)


def fold_rows(x, size):
    return (x[2 * size :] + x[size : 2 * size]) + x[:size]


def cost(flops, nbytes):
    return pl.CostEstimate(flops=int(flops), bytes_accessed=int(nbytes), transcendentals=0)


def array(*shape, dtype=F32):
    return jax.ShapeDtypeStruct(shape, dtype)


def columns(place, unit, start=0, width=None):
    return pl.ds(pl.multiple_of(place * unit + start, STEP), unit if width is None else width)


def unit_places():
    col = lax.axis_index("col")
    i, j = lax.rem(col, 2), lax.div(col, 2)
    k, m = 1 - i, 1 - j
    return {
        "own": (2 * i + j, 4 + 2 * j + i),
        "pass_on": (2 * i + m, 4 + 2 * j + k),
        "away_first": (2 * k + m, 4 + 2 * m + k),
        "away_second": (2 * k + j, 4 + 2 * m + i),
    }


def places_of(*names):
    places = unit_places()
    return [place for name in names for place in places[name]]


def first_kernel(
    total, locked, vectors, mass, out, high, low, mass_out, here_a, here_b, held_buf, new_buf, pieces, acc, sems, more_sems
):
    held, rows = locked.shape
    unit = here_a.shape[1]
    count = rows // CHUNK

    def copies(index):
        span, slot = pl.ds(index * CHUNK, CHUNK), index % SLOTS
        return (
            pltpu.make_async_copy(vectors.at[:, span], new_buf.at[slot], sems.at[0, slot]),
            pltpu.make_async_copy(locked.at[:, span], held_buf.at[slot], sems.at[1, slot]),
        )

    mass_copy = pltpu.make_async_copy(mass, mass_out, more_sems.at[0])
    mass_copy.start()
    for index in range(SLOTS - 1):
        for copy in copies(index):
            copy.start()
    places = places_of("own")
    own_copies = [
        pltpu.make_async_copy(vectors.at[:, columns(place, unit)], here, more_sems.at[1 + which])
        for which, (place, here) in enumerate(zip(places, (here_a, here_b)))
    ]
    mass_copy.wait()
    for index in range(count + 1):
        if index < count:
            if index + SLOTS - 1 < count:
                for copy in copies(index + SLOTS - 1):
                    copy.start()
            if index == count // 2:
                for copy in own_copies:
                    copy.start()
            for copy in copies(index):
                copy.wait()
        if index > 0:
            span = pl.ds((index - 1) * CHUNK, CHUNK)
            left = jnp.concatenate([high[:, span], low[:, span]], axis=0)
            term = dot_nt(left, pieces[(index - 1) % 2])
            if index == 1:
                acc[...] = term
            else:
                acc[...] += term
        if index < count:
            span, slot = pl.ds(index * CHUNK, CHUNK), index % SLOTS
            put_thirds(pieces.at[index % 2], new_buf.at[slot], mass_out[:, span])
            put_halves(high, low, span, held_buf.at[slot])
    for copy in own_copies:
        copy.wait()
    out[...] = fold_rows((acc[:held] + acc[held:]).T, out.shape[0]) * (1.0 / total)


def first_coefficients(locked, vectors, mass, unit, total):
    (held, rows), new = locked.shape, vectors.shape[0]
    in_hbm = [pltpu.with_memory_space_constraint(x, pltpu.HBM) for x in (locked, vectors, mass)]
    return pl.pallas_call(
        functools.partial(first_kernel, total),
        out_shape=[
            array(new, held),
            array(held, rows, dtype=BF16),
            array(held, rows, dtype=BF16),
            array(1, rows),
            array(new, unit),
            array(new, unit),
        ],
        in_specs=[HBM] * 3,
        out_specs=[VMEM] * 6,
        scratch_shapes=[
            pltpu.VMEM((SLOTS, held, CHUNK), F32),
            pltpu.VMEM((SLOTS, new, CHUNK), F32),
            pltpu.VMEM((2, 3 * new, CHUNK), BF16),
            pltpu.VMEM((2 * held, 3 * new), F32),
            pltpu.SemaphoreType.DMA((2, SLOTS)),
            pltpu.SemaphoreType.DMA((3,)),
        ],
        compiler_params=PARAMS,
        cost_estimate=cost(12 * held * new * rows, 8 * held * rows),
    )(*in_hbm)


def fold_gram(x, size):
    part = fold_rows(x, size)
    return (part[:, 2 * size :] + part[:, size : 2 * size]) + part[:, :size]


def second_kernel(count, total, mode, high, low, mass, *refs):
    blocks, rest = refs[:count], refs[count:]
    new, unit = blocks[0].shape
    held = high.shape[0]
    rest, (acc, plain, weighted) = rest[:-3], rest[-3:]
    if mode == "own":
        out, grams = rest
    elif mode == "near":
        base, out, grams = rest
    else:
        base, own_grams, near_grams, out, grams = rest
    parts = {"own": ("own",), "near": NEAR, "far": FAR + ("own",) + NEAR}[mode]
    ids = places_of(*parts)
    for place in range(count):
        span = columns(ids[place], unit)
        put_thirds(weighted.at[place], blocks[place], mass[:, span])
        put_thirds(plain.at[place], blocks[place])
        left = jnp.concatenate([high[:, span], low[:, span], plain[place]], axis=0)
        term = dot_nt(left, weighted[place])
        grams[ids[place] if mode == "far" else place] = fold_gram(term[2 * held :], new)
        if place == 0:
            acc[...] = term[: 2 * held]
        else:
            acc[...] += term[: 2 * held]
    second = fold_rows((acc[:held] + acc[held:]).T, new)
    if mode != "own":
        second = second + base[...]
    if mode != "far":
        out[...] = second
        return
    for place in range(2):
        grams[ids[2 + place]] = own_grams[place]
    for place in range(4):
        grams[ids[4 + place]] = near_grams[place]
    gram = grams[0]
    for place in range(1, 8):
        gram = gram + grams[place]
    out[...] = jnp.concatenate([second, gram, jnp.zeros_like(gram)], axis=1) * (1.0 / total)


def second_coefficients(mode, high, low, mass, blocks, total, *others):
    new, unit = blocks[0].shape
    held, count = high.shape[0], len(blocks)
    pieces = pltpu.VMEM((count, 3 * new, unit), BF16)
    scratch = [pltpu.VMEM((2 * held, 3 * new), F32), pieces, pieces]
    if mode == "far":
        shapes = [array(new, held + 2 * new)]
        scratch.insert(0, pltpu.VMEM((8, new, new), F32))
    else:
        shapes = [array(new, held), array(count, new, new)]
    return pl.pallas_call(
        functools.partial(second_kernel, count, total, mode),
        out_shape=shapes,
        in_specs=[VMEM] * (3 + count + len(others)),
        out_specs=[VMEM] * len(shapes),
        scratch_shapes=scratch,
        compiler_params=PARAMS,
        cost_estimate=cost(14 * held * new * count * unit, 4 * (held + new) * count * unit),
    )(high, low, mass, *blocks, *others)


def corrections_kernel(names, bases, coef, high, low, *refs):
    base, outs = refs[:bases], refs[bases:]
    new, unit = outs[0].shape
    held = high.shape[0]
    pieces = thirds(coef[:, :held])
    pieces = jnp.concatenate([pieces, pieces], axis=1)
    places = places_of(*names)
    for which, place in enumerate(places):
        taken_off = which - (len(places) - bases)
        for start in range(0, unit, STEP):
            span, here = columns(place, unit, start, STEP), pl.ds(start, STEP)
            term = dot_nn(pieces, jnp.concatenate([high[:, span], low[:, span]], axis=0))
            term = fold_rows(term, new)
            outs[which][:, here] = base[taken_off][:, here] - term if taken_off >= 0 else term


def corrections(names, coef, high, low, unit, base=()):
    new, held, count = coef.shape[0], high.shape[0], 2 * len(names)
    return pl.pallas_call(
        functools.partial(corrections_kernel, names, len(base)),
        out_shape=[array(new, unit)] * count,
        in_specs=[VMEM] * (3 + len(base)),
        out_specs=[VMEM] * count,
        compiler_params=PARAMS,
        cost_estimate=cost(12 * held * new * count * unit, 4 * (held + new) * count * unit),
    )(coef, high, low, *base)


def take_off_kernel(*refs):
    for place in range(2):
        refs[6 + place][...] = refs[place][...] - refs[2 + place][...] - refs[4 + place][...]


def eliminate(gram):
    size = gram.shape[0]
    shape = (size, 2 * size)
    rows = lax.broadcasted_iota(jnp.int32, shape, 0)
    lanes = lax.broadcasted_iota(jnp.int32, shape, 1)
    eye = (rows[:, :size] == lanes[:, :size]).astype(F32)
    work = jnp.concatenate([gram, eye], axis=1)
    for start in range(0, size, GROUP):
        group = range(start, start + GROUP)
        column = {k: jnp.broadcast_to(work[:, k : k + 1], shape) for k in group}
        line = {k: work[k : k + 1, :] for k in group}
        for k in group:
            inverse = 1.0 / column[k][k : k + 1, :]
            scaled = line[k] * inverse
            for later in range(k + 1, start + GROUP):
                line[later] = line[later] - column[k][later : later + 1, :] * scaled
                column[later] = column[later] - column[k] * (column[later][k : k + 1, :] * inverse)
            work = work - jnp.where(rows > k, column[k], 0.0) * scaled
    pivots = jnp.sum(jnp.where(lanes == rows, work, 0.0), axis=1, keepdims=True)
    scale = lax.rsqrt(pivots)
    work = work * (scale * (1.5 - 0.5 * pivots * scale * scale))
    upper = jnp.where(lanes >= rows, work, 0.0)[:, :size]
    return upper, work[:, size:]


def spread(matrix):
    pieces = thirds(matrix)
    return jnp.concatenate([pieces, pieces, pieces], axis=1)


def apply_left(spread_matrix, block):
    return fold_rows(dot_nn(spread_matrix, thirds(block)), block.shape[0])


def gram_of(block, mass):
    size = block.shape[0]
    return fold_gram(dot_nt(thirds(block * mass), thirds(block)), size)


def factor_kernel(both, upper_out, inverse_out):
    size = upper_out.shape[0]
    held = both.shape[1] - 2 * size
    upper_out[...], inverse_out[...] = eliminate(both[:, held : held + size])


def middle_kernel(total, mass, inverse, *refs):
    ins, outs = refs[:6], refs[6:]
    new, unit = outs[0].shape
    left = spread(inverse[...])
    places = places_of("own")
    acc = jnp.zeros((new, new), F32)
    for which, place in enumerate(places):
        for start in range(0, unit, STEP):
            span = pl.ds(start, STEP)
            projected = ins[which][:, span] - ins[2 + which][:, span] - ins[4 + which][:, span]
            middle = apply_left(left, projected)
            outs[which][:, span] = middle
            acc = acc + gram_of(middle, mass[:, columns(place, unit, start, STEP)])
    outs[2][...] = acc * (1.0 / total)


def last_kernel(gram, upper_one, factor_out, inverse_out):
    upper, inverse = eliminate(gram[...])
    factor_out[...] = jnp.dot(
        upper, upper_one[...], precision=lax.Precision.HIGHEST, preferred_element_type=F32
    )
    inverse_out[...] = inverse


def finish_kernel(names, inverse, *refs):
    count = 2 * len(names)
    blocks, (out, buf, sems) = refs[:count], refs[-3:]
    unit = blocks[0].shape[1]
    left = spread(inverse[...])
    copies = []
    for which, place in enumerate(places_of(*names)):
        for start in range(0, unit, STEP):
            span = pl.ds(start, STEP)
            buf[which, :, span] = apply_left(left, blocks[which][:, span])
        copy = pltpu.make_async_copy(buf.at[which], out.at[:, columns(place, unit)], sems.at[which])
        copy.start()
        copies.append(copy)
    for copy in copies:
        copy.wait()


def finish(names, inverse, blocks, rows, target=None):
    new, unit = blocks[0].shape
    count = len(blocks)
    extra = [] if target is None else [target]
    return pl.pallas_call(
        functools.partial(finish_kernel, names),
        out_shape=array(new, rows),
        in_specs=[VMEM] * (1 + count) + [HBM] * len(extra),
        out_specs=HBM,
        scratch_shapes=[pltpu.VMEM((count, new, unit), F32), pltpu.SemaphoreType.DMA((count,))],
        input_output_aliases={} if target is None else {1 + count: 0},
        compiler_params=PARAMS,
        cost_estimate=cost(18 * new * new * count * unit, 8 * new * count * unit),
    )(inverse, *blocks, *extra)


def flip(x, axis, bit):
    size = lax.axis_size(axis)
    return lax.ppermute(x, axis, [(i, i ^ bit) for i in range(size)])


def sum_over(x, axis):
    size = lax.axis_size(axis)
    bit = 1
    while bit < size:
        x = x + flip(x, axis, bit)
        bit *= 2
    return x


def local(locked, vectors, mass):
    new, rows = vectors.shape
    total = rows * lax.axis_size("row")
    unit = rows // 8
    first, high, low, mass, *here = first_coefficients(locked, vectors, mass.reshape(1, rows), unit, total)

    def scatter_sum(coef, base):
        a1, b1 = corrections(("away_first",), coef, high, low, unit)
        ra1, rb1 = flip(a1, "col", 1), flip(b1, "col", 2)
        a2, b2 = corrections(("away_second",), coef, high, low, unit)
        ra2, rb2 = flip(a2, "col", 1), flip(b2, "col", 2)
        a3, b3, a4, b4 = corrections(("pass_on", "own"), coef, high, low, unit, base)
        ra3, rb3 = flip(a3 + ra1, "col", 2), flip(b3 + rb1, "col", 1)
        return a4, b4, ra2, rb2, ra3, rb3

    first = sum_over(first, "row")
    once = pl.pallas_call(
        take_off_kernel,
        out_shape=[array(new, unit)] * 2,
        in_specs=[VMEM] * 6,
        out_specs=[VMEM] * 2,
        compiler_params=PARAMS,
        cost_estimate=cost(6 * new * unit, 32 * new * unit),
    )(*scatter_sum(first, here))
    a, b = once
    ay, bx = flip(a, "col", 2), flip(b, "col", 1)
    ax, by = flip(a, "col", 1), flip(b, "col", 2)
    far = flip(ay, "col", 1), flip(bx, "col", 2)
    second, grams = second_coefficients("own", high, low, mass, once, total)
    second, more = second_coefficients("near", high, low, mass, (ay, bx, ax, by), total, second)
    (second,) = second_coefficients("far", high, low, mass, far, total, second, grams, more)
    second = sum_over(second, "row")
    parts = scatter_sum(second, once)

    upper, inverse = pl.pallas_call(
        factor_kernel,
        out_shape=[array(new, new)] * 2,
        in_specs=[VMEM],
        out_specs=[VMEM] * 2,
        compiler_params=PARAMS,
        cost_estimate=cost(1e6, 1e5),
    )(second)
    a, b, gram = pl.pallas_call(
        functools.partial(middle_kernel, total),
        out_shape=[array(new, unit)] * 2 + [array(new, new)],
        in_specs=[VMEM] * 8,
        out_specs=[VMEM] * 3,
        compiler_params=PARAMS,
        cost_estimate=cost(36 * new * new * 2 * unit, 24 * new * unit),
    )(mass, inverse, *parts)
    one, two, three = (flip(gram, "col", n) for n in (1, 2, 3))
    one, two, three, a, b = lax.optimization_barrier((one, two, three, a, b))
    gram = sum_over((gram + one) + (two + three), "row")
    ay, bx = flip(a, "col", 2), flip(b, "col", 1)
    ax, by = flip(a, "col", 1), flip(b, "col", 2)
    far = flip(ay, "col", 1), flip(bx, "col", 2)
    factor, inverse = pl.pallas_call(
        last_kernel,
        out_shape=[array(new, new)] * 2,
        in_specs=[VMEM] * 2,
        out_specs=[VMEM] * 2,
        compiler_params=PARAMS,
        cost_estimate=cost(5e9, 1e5),
    )(gram, upper)
    appended = finish(("own",) + NEAR, inverse, (a, b, ay, bx, ax, by), rows)
    appended = finish(FAR, inverse, far, rows, appended)
    return (appended, factor)


def solution(mesh):
    return jax.shard_map(
        local,
        mesh=mesh,
        in_specs=(P("col", "row"), P(None, "row"), P("row")),
        out_specs=(P(None, "row"), P()),
        check_vma=False,
    )
```

```python
import functools

import jax
import jax.numpy as jnp
from jax import lax
from jax.experimental import pallas as pl
from jax.experimental.pallas import tpu as pltpu
from jax.sharding import PartitionSpec as P

F32 = jnp.float32
BF16 = jnp.bfloat16
STEP = 1024
CHUNK = 2048
SLOTS = 7
ROWS = 16
GROUP = 4
VMEM_LIMIT = 24 * 1024 * 1024
VMEM = pl.BlockSpec(memory_space=pltpu.VMEM)
HBM = pl.BlockSpec(memory_space=pltpu.HBM)
NEAR, FAR = ("pass_on", "away_second"), ("away_first",)
PARAMS = pltpu.CompilerParams(vmem_limit_bytes=VMEM_LIMIT)


def halves(x):
    high = x.astype(BF16)
    return high, (x - high.astype(F32)).astype(BF16)


def thirds(x):
    high = x.astype(BF16)
    rest = x - high.astype(F32)
    middle = rest.astype(BF16)
    low = (rest - middle.astype(F32)).astype(BF16)
    return jnp.concatenate([high, middle, low], axis=0)


def put_halves(high, low, span, source):
    for row in range(0, source.shape[0], ROWS):
        here = pl.ds(row, ROWS)
        high[here, span], low[here, span] = halves(source[here, :])


def put_thirds(target, source, weights=None):
    size = source.shape[0]
    for row in range(0, size, ROWS):
        part = source[pl.ds(row, ROWS), :]
        part = thirds(part if weights is None else part * weights)
        for third in range(3):
            target[pl.ds(third * size + row, ROWS), :] = part[third * ROWS : (third + 1) * ROWS]


def dot_nt(a, b):
    return lax.dot_general(a, b, (((1,), (1,)), ((), ())), preferred_element_type=F32)


def dot_nn(a, b):
    return lax.dot_general(a, b, (((1,), (0,)), ((), ())), preferred_element_type=F32)


def fold_rows(x, size):
    return (x[2 * size :] + x[size : 2 * size]) + x[:size]


def cost(flops, nbytes):
    return pl.CostEstimate(flops=int(flops), bytes_accessed=int(nbytes), transcendentals=0)


def array(*shape, dtype=F32):
    return jax.ShapeDtypeStruct(shape, dtype)


def columns(place, unit, start=0, width=None):
    return pl.ds(pl.multiple_of(place * unit + start, STEP), unit if width is None else width)


def unit_places():
    col = lax.axis_index("col")
    i, j = lax.rem(col, 2), lax.div(col, 2)
    k, m = 1 - i, 1 - j
    return {
        "own": (2 * i + j, 4 + 2 * j + i),
        "pass_on": (2 * i + m, 4 + 2 * j + k),
        "away_first": (2 * k + m, 4 + 2 * m + k),
        "away_second": (2 * k + j, 4 + 2 * m + i),
        "over_x": (2 * k + j, 4 + 2 * j + k),
        "over_y": (2 * i + m, 4 + 2 * m + i),
    }


def places_of(*names):
    places = unit_places()
    return [place for name in names for place in places[name]]


def first_kernel(
    total, locked, vectors, mass, out, high, low, mass_out, here_a, here_b, held_buf, new_buf, pieces, acc, sems, more_sems
):
    held, rows = locked.shape
    unit = here_a.shape[1]
    count = rows // CHUNK

    def copies(index):
        span, slot = pl.ds(index * CHUNK, CHUNK), index % SLOTS
        return (
            pltpu.make_async_copy(vectors.at[:, span], new_buf.at[slot], sems.at[0, slot]),
            pltpu.make_async_copy(locked.at[:, span], held_buf.at[slot], sems.at[1, slot]),
        )

    mass_copy = pltpu.make_async_copy(mass, mass_out, more_sems.at[0])
    mass_copy.start()
    for index in range(min(SLOTS - 1, count)):
        for copy in copies(index):
            copy.start()
    places = places_of("own")
    own_copies = [
        pltpu.make_async_copy(vectors.at[:, columns(place, unit)], here, more_sems.at[1 + which])
        for which, (place, here) in enumerate(zip(places, (here_a, here_b)))
    ]
    mass_copy.wait()
    for index in range(count + 1):
        if index < count:
            if index + SLOTS - 1 < count:
                for copy in copies(index + SLOTS - 1):
                    copy.start()
            if index == count // 2:
                for copy in own_copies:
                    copy.start()
            for copy in copies(index):
                copy.wait()
        if index > 0:
            span = pl.ds((index - 1) * CHUNK, CHUNK)
            left = jnp.concatenate([high[:, span], low[:, span]], axis=0)
            term = dot_nt(left, pieces[(index - 1) % 2])
            if index == 1:
                acc[...] = term
            else:
                acc[...] += term
        if index < count:
            span, slot = pl.ds(index * CHUNK, CHUNK), index % SLOTS
            put_thirds(pieces.at[index % 2], new_buf.at[slot], mass_out[:, span])
            put_halves(high, low, span, held_buf.at[slot])
    for copy in own_copies:
        copy.wait()
    out[...] = fold_rows((acc[:held] + acc[held:]).T, out.shape[0]) * (1.0 / total)


def first_coefficients(locked, vectors, mass, unit, total):
    (held, rows), new = locked.shape, vectors.shape[0]
    slots = min(SLOTS, rows // CHUNK)
    in_hbm = [pltpu.with_memory_space_constraint(x, pltpu.HBM) for x in (locked, vectors, mass)]
    return pl.pallas_call(
        functools.partial(first_kernel, total),
        out_shape=[
            array(new, held),
            array(held, rows, dtype=BF16),
            array(held, rows, dtype=BF16),
            array(1, rows),
            array(new, unit),
            array(new, unit),
        ],
        in_specs=[HBM] * 3,
        out_specs=[VMEM] * 6,
        scratch_shapes=[
            pltpu.VMEM((slots, held, CHUNK), F32),
            pltpu.VMEM((slots, new, CHUNK), F32),
            pltpu.VMEM((2, 3 * new, CHUNK), BF16),
            pltpu.VMEM((2 * held, 3 * new), F32),
            pltpu.SemaphoreType.DMA((2, slots)),
            pltpu.SemaphoreType.DMA((3,)),
        ],
        compiler_params=PARAMS,
        cost_estimate=cost(12 * held * new * rows, 8 * held * rows),
    )(*in_hbm)


def fold_gram(x, size):
    part = fold_rows(x, size)
    return (part[:, 2 * size :] + part[:, size : 2 * size]) + part[:, :size]


def second_kernel(count, total, mode, high, low, mass, *refs):
    blocks, rest = refs[:count], refs[count:]
    new, unit = blocks[0].shape
    held = high.shape[0]
    rest, (acc, plain, weighted) = rest[:-3], rest[-3:]
    if mode == "own":
        out, grams = rest
    elif mode == "near":
        base, out, grams = rest
    else:
        base, own_grams, near_grams, out, grams = rest
    parts = {"own": ("own",), "near": NEAR, "far": FAR + ("own",) + NEAR}[mode]
    ids = places_of(*parts)
    for place in range(count):
        span = columns(ids[place], unit)
        put_thirds(weighted.at[place], blocks[place], mass[:, span])
        put_thirds(plain.at[place], blocks[place])
        left = jnp.concatenate([high[:, span], low[:, span], plain[place]], axis=0)
        term = dot_nt(left, weighted[place])
        grams[ids[place] if mode == "far" else place] = fold_gram(term[2 * held :], new)
        if place == 0:
            acc[...] = term[: 2 * held]
        else:
            acc[...] += term[: 2 * held]
    second = fold_rows((acc[:held] + acc[held:]).T, new)
    if mode != "own":
        second = second + base[...]
    if mode != "far":
        out[...] = second
        return
    for place in range(2):
        grams[ids[2 + place]] = own_grams[place]
    for place in range(4):
        grams[ids[4 + place]] = near_grams[place]
    gram = grams[0]
    for place in range(1, 8):
        gram = gram + grams[place]
    flat = new * new // held
    gram = jnp.concatenate([gram[row : row + flat] for row in range(0, new, flat)], axis=1)
    out[...] = jnp.concatenate([second, gram], axis=0) * (1.0 / total)


def second_coefficients(mode, high, low, mass, blocks, total, *others):
    new, unit = blocks[0].shape
    held, count = high.shape[0], len(blocks)
    pieces = pltpu.VMEM((count, 3 * new, unit), BF16)
    scratch = [pltpu.VMEM((2 * held, 3 * new), F32), pieces, pieces]
    if mode == "far":
        shapes = [array(new + new * new // held, held)]
        scratch.insert(0, pltpu.VMEM((8, new, new), F32))
    else:
        shapes = [array(new, held), array(count, new, new)]
    return pl.pallas_call(
        functools.partial(second_kernel, count, total, mode),
        out_shape=shapes,
        in_specs=[VMEM] * (3 + count + len(others)),
        out_specs=[VMEM] * len(shapes),
        scratch_shapes=scratch,
        compiler_params=PARAMS,
        cost_estimate=cost(14 * held * new * count * unit, 4 * (held + new) * count * unit),
    )(high, low, mass, *blocks, *others)


def corrections_kernel(names, bases, coef, high, low, *refs):
    base, outs = refs[:bases], refs[bases:]
    new, unit = outs[0].shape
    held = high.shape[0]
    pieces = thirds(coef[:new, :])
    pieces = jnp.concatenate([pieces, pieces], axis=1)
    places = places_of(*names)
    for which, place in enumerate(places):
        taken_off = which - (len(places) - bases)
        for start in range(0, unit, STEP):
            span, here = columns(place, unit, start, STEP), pl.ds(start, STEP)
            term = dot_nn(pieces, jnp.concatenate([high[:, span], low[:, span]], axis=0))
            term = fold_rows(term, new)
            outs[which][:, here] = base[taken_off][:, here] - term if taken_off >= 0 else term


def corrections(names, coef, high, low, new, unit, base=()):
    held, count = high.shape[0], 2 * len(names)
    return pl.pallas_call(
        functools.partial(corrections_kernel, names, len(base)),
        out_shape=[array(new, unit)] * count,
        in_specs=[VMEM] * (3 + len(base)),
        out_specs=[VMEM] * count,
        compiler_params=PARAMS,
        cost_estimate=cost(12 * held * new * count * unit, 4 * (held + new) * count * unit),
    )(coef, high, low, *base)


def take_off_kernel(*refs):
    for place in range(2):
        refs[6 + place][...] = refs[place][...] - refs[2 + place][...] - refs[4 + place][...]


def eliminate(gram):
    size = gram.shape[0]
    shape = (size, 2 * size)
    rows = lax.broadcasted_iota(jnp.int32, shape, 0)
    lanes = lax.broadcasted_iota(jnp.int32, shape, 1)
    eye = (rows[:, :size] == lanes[:, :size]).astype(F32)
    work = jnp.concatenate([gram, eye], axis=1)
    for start in range(0, size, GROUP):
        group = range(start, start + GROUP)
        column = {k: jnp.broadcast_to(work[:, k : k + 1], shape) for k in group}
        line = {k: work[k : k + 1, :] for k in group}
        for k in group:
            inverse = 1.0 / column[k][k : k + 1, :]
            scaled = line[k] * inverse
            for later in range(k + 1, start + GROUP):
                line[later] = line[later] - column[k][later : later + 1, :] * scaled
                column[later] = column[later] - column[k] * (column[later][k : k + 1, :] * inverse)
            work = work - jnp.where(rows > k, column[k], 0.0) * scaled
    pivots = jnp.sum(jnp.where(lanes == rows, work, 0.0), axis=1, keepdims=True)
    scale = lax.rsqrt(pivots)
    work = work * (scale * (1.5 - 0.5 * pivots * scale * scale))
    upper = jnp.where(lanes >= rows, work, 0.0)[:, :size]
    return upper, work[:, size:]


def spread(matrix):
    pieces = thirds(matrix)
    return jnp.concatenate([pieces, pieces, pieces], axis=1)


def apply_left(spread_matrix, block):
    return fold_rows(dot_nn(spread_matrix, thirds(block)), block.shape[0])


def gram_of(block, mass):
    size = block.shape[0]
    return fold_gram(dot_nt(thirds(block * mass), thirds(block)), size)


def factor_kernel(both, upper_out, inverse_out):
    size = upper_out.shape[0]
    packed = both[size:, :]
    gram = jnp.concatenate([packed[:, lane : lane + size] for lane in range(0, packed.shape[1], size)], axis=0)
    upper_out[...], inverse_out[...] = eliminate(gram)


def middle_kernel(total, mass, inverse, *refs):
    ins, outs = refs[:6], refs[6:]
    new, unit = ins[0].shape
    left = spread(inverse[...])
    places = places_of("own")
    acc = jnp.zeros((new, new), F32)
    for which, place in enumerate(places):
        for start in range(0, unit, STEP):
            span = pl.ds(start, STEP)
            projected = ins[which][:, span] - ins[2 + which][:, span] - ins[4 + which][:, span]
            middle = apply_left(left, projected)
            outs[0][pl.ds(which * new, new), span] = middle
            acc = acc + gram_of(middle, mass[:, columns(place, unit, start, STEP)])
    outs[1][...] = acc * (1.0 / total)


def last_kernel(gram, upper_one, factor_out, inverse_out):
    upper, inverse = eliminate(gram[...])
    factor_out[...] = jnp.dot(
        upper, upper_one[...], precision=lax.Precision.HIGHEST, preferred_element_type=F32
    )
    inverse_out[...] = inverse


def finish_kernel(order, given, inverse, *refs):
    blocks, (out, buf, sems) = refs[:given], refs[-3:]
    new, unit = buf.shape[1:]
    left = spread(inverse[...])
    stack = blocks[0].shape[0] // new
    copies = []
    for which, place in enumerate(places_of(*order)):
        rows = pl.ds(which % stack * new, new)
        for start in range(0, unit, STEP):
            span = pl.ds(start, STEP)
            buf[which, :, span] = apply_left(left, blocks[which // stack][rows, span])
        copy = pltpu.make_async_copy(buf.at[which], out.at[:, columns(place, unit)], sems.at[which])
        copy.start()
        copies.append(copy)
    for copy in copies:
        copy.wait()


def finish(order, inverse, blocks, new, rows, target=None):
    unit = blocks[0].shape[1]
    given, count = len(blocks), len(blocks) * blocks[0].shape[0] // new
    extra = [] if target is None else [target]
    return pl.pallas_call(
        functools.partial(finish_kernel, order, given),
        out_shape=array(new, rows),
        in_specs=[VMEM] * (1 + given) + [HBM] * len(extra),
        out_specs=HBM,
        scratch_shapes=[pltpu.VMEM((count, new, unit), F32), pltpu.SemaphoreType.DMA((count,))],
        input_output_aliases={} if target is None else {1 + given: 0},
        compiler_params=PARAMS,
        cost_estimate=cost(18 * new * new * count * unit, 8 * new * count * unit),
    )(inverse, *blocks, *extra)


def flip(x, axis, bit):
    size = lax.axis_size(axis)
    return lax.ppermute(x, axis, [(i, i ^ bit) for i in range(size)])


def sum_over(x, axis):
    size = lax.axis_size(axis)
    bit = 1
    while bit < size:
        x = x + flip(x, axis, bit)
        bit *= 2
    return x


def local(locked, vectors, mass):
    new, rows = vectors.shape
    total = rows * lax.axis_size("row")
    unit = rows // 8
    first, high, low, mass, *here = first_coefficients(locked, vectors, mass.reshape(1, rows), unit, total)

    def scatter_sum(coef, base):
        a1, b1 = corrections(("away_first",), coef, high, low, new, unit)
        ra1, rb1 = flip(a1, "col", 1), flip(b1, "col", 2)
        a2, b2 = corrections(("away_second",), coef, high, low, new, unit)
        ra2, rb2 = flip(a2, "col", 1), flip(b2, "col", 2)
        a3, b3, a4, b4 = corrections(("pass_on", "own"), coef, high, low, new, unit, base)
        ra3, rb3 = flip(a3 + ra1, "col", 2), flip(b3 + rb1, "col", 1)
        return a4, b4, ra2, rb2, ra3, rb3

    first = sum_over(first, "row")
    once = pl.pallas_call(
        take_off_kernel,
        out_shape=[array(new, unit)] * 2,
        in_specs=[VMEM] * 6,
        out_specs=[VMEM] * 2,
        compiler_params=PARAMS,
        cost_estimate=cost(6 * new * unit, 32 * new * unit),
    )(*scatter_sum(first, here))
    a, b = once
    ay, bx = flip(a, "col", 2), flip(b, "col", 1)
    ax, by = flip(a, "col", 1), flip(b, "col", 2)
    far = flip(ay, "col", 1), flip(bx, "col", 2)
    second, grams = second_coefficients("own", high, low, mass, once, total)
    second, more = second_coefficients("near", high, low, mass, (ay, bx, ax, by), total, second)
    (second,) = second_coefficients("far", high, low, mass, far, total, second, grams, more)
    second = sum_over(second, "row")
    parts = scatter_sum(second, once)

    upper, inverse = pl.pallas_call(
        factor_kernel,
        out_shape=[array(new, new)] * 2,
        in_specs=[VMEM],
        out_specs=[VMEM] * 2,
        compiler_params=PARAMS,
        cost_estimate=cost(1e6, 1e5),
    )(second)
    pair, gram = pl.pallas_call(
        functools.partial(middle_kernel, total),
        out_shape=[array(2 * new, unit), array(new, new)],
        in_specs=[VMEM] * 8,
        out_specs=[VMEM] * 2,
        compiler_params=PARAMS,
        cost_estimate=cost(36 * new * new * 2 * unit, 24 * new * unit),
    )(mass, inverse, *parts)
    over_x, over_y = flip(pair, "col", 1), flip(pair, "col", 2)
    gram = sum_over(gram, "row")
    one, two, three = (flip(gram, "col", n) for n in (1, 2, 3))
    one, two, three, ay, bx = lax.optimization_barrier((one, two, three, over_y[:new], over_x[new:]))
    gram = (gram + one) + (two + three)
    far = flip(ay, "col", 1), flip(bx, "col", 2)
    factor, inverse = pl.pallas_call(
        last_kernel,
        out_shape=[array(new, new)] * 2,
        in_specs=[VMEM] * 2,
        out_specs=[VMEM] * 2,
        compiler_params=PARAMS,
        cost_estimate=cost(5e9, 1e5),
    )(gram, upper)
    appended = finish(("own", "over_x", "over_y"), inverse, (pair, over_x, over_y), new, rows)
    appended = finish(FAR, inverse, far, new, rows, appended)
    return (appended, factor)


def solution(mesh):
    return jax.shard_map(
        local,
        mesh=mesh,
        in_specs=(P("col", "row"), P(None, "row"), P("row")),
        out_specs=(P(None, "row"), P()),
        check_vma=False,
    )
```

```python
import functools

import jax
import jax.numpy as jnp
from jax import lax
from jax.experimental import pallas as pl
from jax.experimental.pallas import tpu as pltpu
from jax.sharding import PartitionSpec as P

F32 = jnp.float32
BF16 = jnp.bfloat16
STEP = 1024
SLOTS = 4
ROWS = 16
GROUP = 4
VMEM_LIMIT = 24 * 1024 * 1024
VMEM = pl.BlockSpec(memory_space=pltpu.VMEM)
HBM = pl.BlockSpec(memory_space=pltpu.HBM)
NEAR, FAR = ("pass_on", "away_second"), ("away_first",)
PARAMS = pltpu.CompilerParams(vmem_limit_bytes=VMEM_LIMIT)


def halves(x):
    high = x.astype(BF16)
    return high, (x - high.astype(F32)).astype(BF16)


def thirds(x):
    high = x.astype(BF16)
    rest = x - high.astype(F32)
    middle = rest.astype(BF16)
    low = (rest - middle.astype(F32)).astype(BF16)
    return jnp.concatenate([high, middle, low], axis=0)


def put_halves(high, low, span, source):
    for row in range(0, source.shape[0], ROWS):
        here = pl.ds(row, ROWS)
        high[here, span], low[here, span] = halves(source[here, :])


def put_pieces(target, source, weights=None):
    size = source.shape[0]
    count = target.shape[0] // size
    for row in range(0, size, ROWS):
        rest = source[pl.ds(row, ROWS), :]
        rest = rest if weights is None else rest * weights
        for piece in range(count):
            part = rest.astype(BF16)
            target[pl.ds(piece * size + row, ROWS), :] = part
            if piece + 1 < count:
                rest = rest - part.astype(F32)


def dot_nt(a, b):
    return lax.dot_general(a, b, (((1,), (1,)), ((), ())), preferred_element_type=F32)


def dot_nn(a, b):
    return lax.dot_general(a, b, (((1,), (0,)), ((), ())), preferred_element_type=F32)


def fold_rows(x, size):
    return (x[2 * size :] + x[size : 2 * size]) + x[:size]


def cost(flops, nbytes):
    return pl.CostEstimate(flops=int(flops), bytes_accessed=int(nbytes), transcendentals=0)


def array(*shape, dtype=F32):
    return jax.ShapeDtypeStruct(shape, dtype)


def columns(place, unit, start=0, width=None):
    return pl.ds(pl.multiple_of(place * unit + start, STEP), unit if width is None else width)


def unit_places():
    col = lax.axis_index("col")
    i, j = lax.rem(col, 2), lax.div(col, 2)
    k, m = 1 - i, 1 - j
    return {
        "own": (2 * i + j, 4 + 2 * j + i),
        "pass_on": (2 * i + m, 4 + 2 * j + k),
        "away_first": (2 * k + m, 4 + 2 * m + k),
        "away_second": (2 * k + j, 4 + 2 * m + i),
        "over_x": (2 * k + j, 4 + 2 * j + k),
        "over_y": (2 * i + m, 4 + 2 * m + i),
    }


def places_of(*names):
    places = unit_places()
    return [place for name in names for place in places[name]]


def first_kernel(
    total, locked, vectors, mass, out, he, ho, le, lo, mass_out, here_a, here_b, held_buf, new_buf, pe, po, acc, sems, more_sems
):
    held, rows = locked.shape
    unit = here_a.shape[1]
    chunk = unit // 2
    count = rows // chunk
    high, low, pieces = (he, ho), (le, lo), (pe, po)

    def copies(index):
        span, slot = pl.ds(index * chunk, chunk), index % SLOTS
        return (
            pltpu.make_async_copy(vectors.at[:, span], new_buf.at[slot], sems.at[0, slot]),
            pltpu.make_async_copy(locked.at[:, span], held_buf.at[slot], sems.at[1, slot]),
        )

    mass_copy = pltpu.make_async_copy(mass, mass_out, more_sems.at[0])
    mass_copy.start()
    for index in range(min(SLOTS - 1, count)):
        for copy in copies(index):
            copy.start()
    places = places_of("own")
    own_copies = [
        pltpu.make_async_copy(vectors.at[:, columns(place, unit)], here, more_sems.at[1 + which])
        for which, (place, here) in enumerate(zip(places, (here_a, here_b)))
    ]
    mass_copy.wait()
    for index in range(count + 1):
        if index < count:
            if index + SLOTS - 1 < count:
                for copy in copies(index + SLOTS - 1):
                    copy.start()
            if index == count // 2:
                for copy in own_copies:
                    copy.start()
            for copy in copies(index):
                copy.wait()
        if index > 0:
            half, span = (index - 1) % 2, pl.ds((index - 1) // 2 * chunk, chunk)
            left = jnp.concatenate([high[half][:, span], low[half][:, span]], axis=0)
            term = dot_nt(left, pieces[half][...])
            if index == 1:
                acc[...] = term
            else:
                acc[...] += term
        if index < count:
            half, slot = index % 2, index % SLOTS
            put_pieces(pieces[half], new_buf.at[slot], mass_out[:, pl.ds(index * chunk, chunk)])
            put_halves(high[half], low[half], pl.ds(index // 2 * chunk, chunk), held_buf.at[slot])
    for copy in own_copies:
        copy.wait()
    both = (acc[held:] + acc[:held]).T
    new = out.shape[0]
    out[...] = (both[new:] + both[:new]) * (1.0 / total)


def first_coefficients(locked, vectors, mass, unit, total):
    (held, rows), new = locked.shape, vectors.shape[0]
    chunk = unit // 2
    slots = min(SLOTS, rows // chunk)
    in_hbm = [pltpu.with_memory_space_constraint(x, pltpu.HBM) for x in (locked, vectors, mass)]
    return pl.pallas_call(
        functools.partial(first_kernel, total),
        out_shape=[
            array(new, held),
            *[array(held, rows // 2, dtype=BF16)] * 4,
            array(1, rows),
            array(new, unit),
            array(new, unit),
        ],
        in_specs=[HBM] * 3,
        out_specs=[VMEM] * 8,
        scratch_shapes=[
            pltpu.VMEM((slots, held, chunk), F32),
            pltpu.VMEM((slots, new, chunk), F32),
            pltpu.VMEM((2 * new, chunk), BF16),
            pltpu.VMEM((2 * new, chunk), BF16),
            pltpu.VMEM((2 * held, 2 * new), F32),
            pltpu.SemaphoreType.DMA((2, slots)),
            pltpu.SemaphoreType.DMA((3,)),
        ],
        compiler_params=PARAMS,
        cost_estimate=cost(12 * held * new * rows, 8 * held * rows),
    )(*in_hbm)


def fold_gram(x, size):
    part = fold_rows(x, size)
    return (part[:, 2 * size :] + part[:, size : 2 * size]) + part[:, :size]


def second_kernel(count, total, mode, he, ho, le, lo, mass, *refs):
    blocks, rest = refs[:count], refs[count:]
    new, unit = blocks[0].shape
    held = he.shape[0]
    rest, (acc, plain, weighted) = rest[:-3], rest[-3:]
    if mode == "own":
        out, grams = rest
    elif mode == "near":
        base, out, grams = rest
    else:
        base, own_grams, near_grams, out, grams = rest
    parts = {"own": ("own",), "near": NEAR, "far": FAR + ("own",) + NEAR}[mode]
    ids = places_of(*parts)
    for place in range(count):
        put_pieces(weighted.at[place], blocks[place], mass[:, columns(ids[place], unit)])
        put_pieces(plain.at[place], blocks[place])
        span = columns(ids[place], unit // 2)
        high = jnp.concatenate([he[:, span], ho[:, span]], axis=1)
        low = jnp.concatenate([le[:, span], lo[:, span]], axis=1)
        left = jnp.concatenate([high, low, plain[place]], axis=0)
        term = dot_nt(left, weighted[place])
        grams[ids[place] if mode == "far" else place] = fold_gram(term[2 * held :], new)
        if place == 0:
            acc[...] = term[: 2 * held]
        else:
            acc[...] += term[: 2 * held]
    second = fold_rows((acc[:held] + acc[held:]).T, new)
    if mode != "own":
        second = second + base[...]
    if mode != "far":
        out[...] = second
        return
    for place in range(2):
        grams[ids[2 + place]] = own_grams[place]
    for place in range(4):
        grams[ids[4 + place]] = near_grams[place]
    gram = grams[0]
    for place in range(1, 8):
        gram = gram + grams[place]
    flat = new * new // held
    gram = jnp.concatenate([gram[row : row + flat] for row in range(0, new, flat)], axis=1)
    out[...] = jnp.concatenate([second, gram], axis=0) * (1.0 / total)


def second_coefficients(mode, split, mass, blocks, total, *others):
    new, unit = blocks[0].shape
    held, count = split[0].shape[0], len(blocks)
    pieces = pltpu.VMEM((count, 3 * new, unit), BF16)
    scratch = [pltpu.VMEM((2 * held, 3 * new), F32), pieces, pieces]
    if mode == "far":
        shapes = [array(new + new * new // held, held)]
        scratch.insert(0, pltpu.VMEM((8, new, new), F32))
    else:
        shapes = [array(new, held), array(count, new, new)]
    return pl.pallas_call(
        functools.partial(second_kernel, count, total, mode),
        out_shape=shapes,
        in_specs=[VMEM] * (5 + count + len(others)),
        out_specs=[VMEM] * len(shapes),
        scratch_shapes=scratch,
        compiler_params=PARAMS,
        cost_estimate=cost(14 * held * new * count * unit, 4 * (held + new) * count * unit),
    )(*split, mass, *blocks, *others)


def corrections_kernel(names, bases, coef, he, ho, le, lo, *refs):
    base, outs = refs[:bases], refs[bases:]
    new, unit = outs[0].shape
    half = unit // 2
    pieces = thirds(coef[:new, :])
    pieces = jnp.concatenate([pieces, pieces], axis=1)
    places = places_of(*names)
    for which, place in enumerate(places):
        taken_off = which - (len(places) - bases)
        for start in range(0, unit, STEP):
            span, here = columns(place, half, start % half, STEP), pl.ds(start, STEP)
            high, low = (he, le) if start < half else (ho, lo)
            term = dot_nn(pieces, jnp.concatenate([high[:, span], low[:, span]], axis=0))
            term = fold_rows(term, new)
            outs[which][:, here] = base[taken_off][:, here] - term if taken_off >= 0 else term


def corrections(names, coef, split, new, unit, base=()):
    held, count = split[0].shape[0], 2 * len(names)
    return pl.pallas_call(
        functools.partial(corrections_kernel, names, len(base)),
        out_shape=[array(new, unit)] * count,
        in_specs=[VMEM] * (5 + len(base)),
        out_specs=[VMEM] * count,
        compiler_params=PARAMS,
        cost_estimate=cost(12 * held * new * count * unit, 4 * (held + new) * count * unit),
    )(coef, *split, *base)


def take_off_kernel(*refs):
    for place in range(2):
        refs[6 + place][...] = refs[place][...] - refs[2 + place][...] - refs[4 + place][...]


def eliminate(gram):
    size = gram.shape[0]
    shape = (size, 2 * size)
    rows = lax.broadcasted_iota(jnp.int32, shape, 0)
    lanes = lax.broadcasted_iota(jnp.int32, shape, 1)
    eye = (rows[:, :size] == lanes[:, :size]).astype(F32)
    work = jnp.concatenate([gram, eye], axis=1)
    for start in range(0, size, GROUP):
        group = range(start, start + GROUP)
        column = {k: jnp.broadcast_to(work[:, k : k + 1], shape) for k in group}
        line = {k: work[k : k + 1, :] for k in group}
        for k in group:
            inverse = 1.0 / column[k][k : k + 1, :]
            scaled = line[k] * inverse
            for later in range(k + 1, start + GROUP):
                line[later] = line[later] - column[k][later : later + 1, :] * scaled
                column[later] = column[later] - column[k] * (column[later][k : k + 1, :] * inverse)
            work = work - jnp.where(rows > k, column[k], 0.0) * scaled
    pivots = jnp.sum(jnp.where(lanes == rows, work, 0.0), axis=1, keepdims=True)
    scale = lax.rsqrt(pivots)
    work = work * (scale * (1.5 - 0.5 * pivots * scale * scale))
    upper = jnp.where(lanes >= rows, work, 0.0)[:, :size]
    return upper, work[:, size:]


def spread(matrix):
    pieces = thirds(matrix)
    return jnp.concatenate([pieces, pieces, pieces], axis=1)


def apply_left(spread_matrix, block):
    return fold_rows(dot_nn(spread_matrix, thirds(block)), block.shape[0])


def gram_of(block, mass):
    size = block.shape[0]
    return fold_gram(dot_nt(thirds(block * mass), thirds(block)), size)


def factor_kernel(both, upper_out, inverse_out):
    size = upper_out.shape[0]
    packed = both[size:, :]
    gram = jnp.concatenate([packed[:, lane : lane + size] for lane in range(0, packed.shape[1], size)], axis=0)
    upper_out[...], inverse_out[...] = eliminate(gram)


def middle_kernel(total, mass, inverse, *refs):
    ins, outs = refs[:6], refs[6:]
    new, unit = ins[0].shape
    left = spread(inverse[...])
    places = places_of("own")
    acc = jnp.zeros((new, new), F32)
    for which, place in enumerate(places):
        for start in range(0, unit, STEP):
            span = pl.ds(start, STEP)
            projected = ins[which][:, span] - ins[2 + which][:, span] - ins[4 + which][:, span]
            middle = apply_left(left, projected)
            outs[0][pl.ds(which * new, new), span] = middle
            acc = acc + gram_of(middle, mass[:, columns(place, unit, start, STEP)])
    outs[1][...] = acc * (1.0 / total)


def last_kernel(gram, upper_one, factor_out, inverse_out):
    upper, inverse = eliminate(gram[...])
    factor_out[...] = jnp.dot(
        upper, upper_one[...], precision=lax.Precision.HIGHEST, preferred_element_type=F32
    )
    inverse_out[...] = inverse


def finish_kernel(order, given, inverse, *refs):
    blocks, (out, buf, sems) = refs[:given], refs[-3:]
    new, unit = buf.shape[1:]
    left = spread(inverse[...])
    stack = blocks[0].shape[0] // new
    copies = []
    for which, place in enumerate(places_of(*order)):
        rows = pl.ds(which % stack * new, new)
        for start in range(0, unit, STEP):
            span = pl.ds(start, STEP)
            buf[which, :, span] = apply_left(left, blocks[which // stack][rows, span])
        copy = pltpu.make_async_copy(buf.at[which], out.at[:, columns(place, unit)], sems.at[which])
        copy.start()
        copies.append(copy)
    for copy in copies:
        copy.wait()


def finish(order, inverse, blocks, new, rows, target=None):
    unit = blocks[0].shape[1]
    given, count = len(blocks), len(blocks) * blocks[0].shape[0] // new
    extra = [] if target is None else [target]
    return pl.pallas_call(
        functools.partial(finish_kernel, order, given),
        out_shape=array(new, rows),
        in_specs=[VMEM] * (1 + given) + [HBM] * len(extra),
        out_specs=HBM,
        scratch_shapes=[pltpu.VMEM((count, new, unit), F32), pltpu.SemaphoreType.DMA((count,))],
        input_output_aliases={} if target is None else {1 + given: 0},
        compiler_params=PARAMS,
        cost_estimate=cost(18 * new * new * count * unit, 8 * new * count * unit),
    )(inverse, *blocks, *extra)


def flip(x, axis, bit):
    size = lax.axis_size(axis)
    return lax.ppermute(x, axis, [(i, i ^ bit) for i in range(size)])


def sum_over(x, axis):
    size = lax.axis_size(axis)
    bit = 1
    while bit < size:
        x = x + flip(x, axis, bit)
        bit *= 2
    return x


def local(locked, vectors, mass):
    new, rows = vectors.shape
    total = rows * lax.axis_size("row")
    unit = rows // 8
    first, *split, mass, here_a, here_b = first_coefficients(locked, vectors, mass.reshape(1, rows), unit, total)

    def scatter_sum(coef, base):
        a1, b1 = corrections(("away_first",), coef, split, new, unit)
        ra1, rb1 = flip(a1, "col", 1), flip(b1, "col", 2)
        a2, b2 = corrections(("away_second",), coef, split, new, unit)
        ra2, rb2 = flip(a2, "col", 1), flip(b2, "col", 2)
        a3, b3, a4, b4 = corrections(("pass_on", "own"), coef, split, new, unit, base)
        ra3, rb3 = flip(a3 + ra1, "col", 2), flip(b3 + rb1, "col", 1)
        return a4, b4, ra2, rb2, ra3, rb3

    first = sum_over(first, "row")
    once = pl.pallas_call(
        take_off_kernel,
        out_shape=[array(new, unit)] * 2,
        in_specs=[VMEM] * 6,
        out_specs=[VMEM] * 2,
        compiler_params=PARAMS,
        cost_estimate=cost(6 * new * unit, 32 * new * unit),
    )(*scatter_sum(first, (here_a, here_b)))
    a, b = once
    ay, bx = flip(a, "col", 2), flip(b, "col", 1)
    ax, by = flip(a, "col", 1), flip(b, "col", 2)
    far = flip(ay, "col", 1), flip(bx, "col", 2)
    second, grams = second_coefficients("own", split, mass, once, total)
    second, more = second_coefficients("near", split, mass, (ay, bx, ax, by), total, second)
    (second,) = second_coefficients("far", split, mass, far, total, second, grams, more)
    second = sum_over(second, "row")
    parts = scatter_sum(second, once)

    upper, inverse = pl.pallas_call(
        factor_kernel,
        out_shape=[array(new, new)] * 2,
        in_specs=[VMEM],
        out_specs=[VMEM] * 2,
        compiler_params=PARAMS,
        cost_estimate=cost(1e6, 1e5),
    )(second)
    pair, gram = pl.pallas_call(
        functools.partial(middle_kernel, total),
        out_shape=[array(2 * new, unit), array(new, new)],
        in_specs=[VMEM] * 8,
        out_specs=[VMEM] * 2,
        compiler_params=PARAMS,
        cost_estimate=cost(36 * new * new * 2 * unit, 24 * new * unit),
    )(mass, inverse, *parts)
    over_x, over_y = flip(pair, "col", 1), flip(pair, "col", 2)
    gram = sum_over(gram, "row")
    one, two, three = (flip(gram, "col", n) for n in (1, 2, 3))
    gram = (gram + one) + (two + three)
    far = flip(over_y[:new], "col", 1), flip(over_x[new:], "col", 2)
    factor, inverse = pl.pallas_call(
        last_kernel,
        out_shape=[array(new, new)] * 2,
        in_specs=[VMEM] * 2,
        out_specs=[VMEM] * 2,
        compiler_params=PARAMS,
        cost_estimate=cost(5e9, 1e5),
    )(gram, upper)
    appended = finish(("own", "over_x", "over_y"), inverse, (pair, over_x, over_y), new, rows)
    appended = finish(FAR, inverse, far, new, rows, appended)
    return (appended, factor)


def solution(mesh):
    return jax.shard_map(
        local,
        mesh=mesh,
        in_specs=(P("col", "row"), P(None, "row"), P("row")),
        out_specs=(P(None, "row"), P()),
        check_vma=False,
    )
```

```python
import functools

import jax
import jax.numpy as jnp
from jax import lax
from jax.experimental import pallas as pl
from jax.experimental.pallas import tpu as pltpu
from jax.sharding import PartitionSpec as P

F32 = jnp.float32
BF16 = jnp.bfloat16
STEP = 1024
SLOTS = 4
ROWS = 16
GROUP = 4
VMEM_LIMIT = 24 * 1024 * 1024
VMEM = pl.BlockSpec(memory_space=pltpu.VMEM)
HBM = pl.BlockSpec(memory_space=pltpu.HBM)
NEAR, FAR = ("pass_on", "away_second"), ("away_first",)
PARAMS = pltpu.CompilerParams(vmem_limit_bytes=VMEM_LIMIT)


def halves(x):
    high = x.astype(BF16)
    return high, (x - high.astype(F32)).astype(BF16)


def thirds(x):
    high = x.astype(BF16)
    rest = x - high.astype(F32)
    middle = rest.astype(BF16)
    low = (rest - middle.astype(F32)).astype(BF16)
    return jnp.concatenate([high, middle, low], axis=0)


def put_halves(high, low, span, source):
    for row in range(0, source.shape[0], ROWS):
        here = pl.ds(row, ROWS)
        high[here, span], low[here, span] = halves(source[here, :])


def put_pieces(target, source, weights=None):
    size = source.shape[0]
    count = target.shape[0] // size
    for row in range(0, size, ROWS):
        rest = source[pl.ds(row, ROWS), :]
        rest = rest if weights is None else rest * weights
        for piece in range(count):
            part = rest.astype(BF16)
            target[pl.ds(piece * size + row, ROWS), :] = part
            if piece + 1 < count:
                rest = rest - part.astype(F32)


def dot_nt(a, b):
    return lax.dot_general(a, b, (((1,), (1,)), ((), ())), preferred_element_type=F32)


def dot_nn(a, b):
    return lax.dot_general(a, b, (((1,), (0,)), ((), ())), preferred_element_type=F32)


def fold_rows(x, size):
    return (x[2 * size :] + x[size : 2 * size]) + x[:size]


def cost(flops, nbytes):
    return pl.CostEstimate(flops=int(flops), bytes_accessed=int(nbytes), transcendentals=0)


def array(*shape, dtype=F32):
    return jax.ShapeDtypeStruct(shape, dtype)


def columns(place, unit, start=0, width=None):
    return pl.ds(pl.multiple_of(place * unit + start, STEP), unit if width is None else width)


def unit_places():
    col = lax.axis_index("col")
    i, j = lax.rem(col, 2), lax.div(col, 2)
    k, m = 1 - i, 1 - j
    return {
        "own": (2 * i + j, 4 + 2 * j + i),
        "pass_on": (2 * i + m, 4 + 2 * j + k),
        "away_first": (2 * k + m, 4 + 2 * m + k),
        "away_second": (2 * k + j, 4 + 2 * m + i),
        "over_x": (2 * k + j, 4 + 2 * j + k),
        "over_y": (2 * i + m, 4 + 2 * m + i),
    }


def places_of(*names):
    places = unit_places()
    return [place for name in names for place in places[name]]


def first_kernel(
    total, locked, vectors, mass, out, he, ho, le, lo, mass_out, here_a, here_b, held_buf, new_buf, pe, po, acc, sems, more_sems
):
    held, rows = locked.shape
    unit = here_a.shape[1]
    chunk = unit // 2
    count = rows // chunk
    high, low, pieces = (he, ho), (le, lo), (pe, po)

    def copies(index):
        span, slot = pl.ds(index * chunk, chunk), index % SLOTS
        return (
            pltpu.make_async_copy(vectors.at[:, span], new_buf.at[slot], sems.at[0, slot]),
            pltpu.make_async_copy(locked.at[:, span], held_buf.at[slot], sems.at[1, slot]),
        )

    mass_copy = pltpu.make_async_copy(mass, mass_out, more_sems.at[0])
    mass_copy.start()
    for index in range(min(SLOTS - 1, count)):
        for copy in copies(index):
            copy.start()
    places = places_of("own")
    own_copies = [
        pltpu.make_async_copy(vectors.at[:, columns(place, unit)], here, more_sems.at[1 + which])
        for which, (place, here) in enumerate(zip(places, (here_a, here_b)))
    ]
    mass_copy.wait()
    for index in range(count + 1):
        if index < count:
            if index + SLOTS - 1 < count:
                for copy in copies(index + SLOTS - 1):
                    copy.start()
            if index == count // 2:
                for copy in own_copies:
                    copy.start()
            for copy in copies(index):
                copy.wait()
        if index < count:
            half, slot = index % 2, index % SLOTS
            put_pieces(pieces[half], new_buf.at[slot], mass_out[:, pl.ds(index * chunk, chunk)])
            put_halves(high[half], low[half], pl.ds(index // 2 * chunk, chunk), held_buf.at[slot])
        if index > 0:
            half, span = (index - 1) % 2, pl.ds((index - 1) // 2 * chunk, chunk)
            left = jnp.concatenate([high[half][:, span], low[half][:, span]], axis=0)
            term = dot_nt(left, pieces[half][...])
            if index == 1:
                acc[...] = term
            else:
                acc[...] += term
    for copy in own_copies:
        copy.wait()
    both = (acc[held:] + acc[:held]).T
    new = out.shape[0]
    out[...] = (both[new:] + both[:new]) * (1.0 / total)


def first_coefficients(locked, vectors, mass, unit, total):
    (held, rows), new = locked.shape, vectors.shape[0]
    chunk = unit // 2
    slots = min(SLOTS, rows // chunk)
    in_hbm = [pltpu.with_memory_space_constraint(x, pltpu.HBM) for x in (locked, vectors, mass)]
    return pl.pallas_call(
        functools.partial(first_kernel, total),
        out_shape=[
            array(new, held),
            *[array(held, rows // 2, dtype=BF16)] * 4,
            array(1, rows),
            array(new, unit),
            array(new, unit),
        ],
        in_specs=[HBM] * 3,
        out_specs=[VMEM] * 8,
        scratch_shapes=[
            pltpu.VMEM((slots, held, chunk), F32),
            pltpu.VMEM((slots, new, chunk), F32),
            pltpu.VMEM((2 * new, chunk), BF16),
            pltpu.VMEM((2 * new, chunk), BF16),
            pltpu.VMEM((2 * held, 2 * new), F32),
            pltpu.SemaphoreType.DMA((2, slots)),
            pltpu.SemaphoreType.DMA((3,)),
        ],
        compiler_params=PARAMS,
        cost_estimate=cost(12 * held * new * rows, 8 * held * rows),
    )(*in_hbm)


def fold_gram(x, size):
    part = fold_rows(x, size)
    return (part[:, 2 * size :] + part[:, size : 2 * size]) + part[:, :size]


def second_kernel(count, total, mode, he, ho, le, lo, mass, *refs):
    blocks, rest = refs[:count], refs[count:]
    new, unit = blocks[0].shape
    held = he.shape[0]
    rest, (acc, plain, weighted) = rest[:-3], rest[-3:]
    if mode == "own":
        out, grams = rest
    elif mode == "near":
        base, out, grams = rest
    else:
        base, own_grams, near_grams, out, grams = rest
    parts = {"own": ("own",), "near": NEAR, "far": FAR + ("own",) + NEAR}[mode]
    ids = places_of(*parts)
    for place in range(count):
        put_pieces(weighted.at[place], blocks[place], mass[:, columns(ids[place], unit)])
        put_pieces(plain.at[place], blocks[place])
        span = columns(ids[place], unit // 2)
        high = jnp.concatenate([he[:, span], ho[:, span]], axis=1)
        low = jnp.concatenate([le[:, span], lo[:, span]], axis=1)
        left = jnp.concatenate([high, low, plain[place]], axis=0)
        term = dot_nt(left, weighted[place])
        grams[ids[place] if mode == "far" else place] = fold_gram(term[2 * held :], new)
        if place == 0:
            acc[...] = term[: 2 * held]
        else:
            acc[...] += term[: 2 * held]
    second = fold_rows((acc[:held] + acc[held:]).T, new)
    if mode != "own":
        second = second + base[...]
    if mode != "far":
        out[...] = second
        return
    for place in range(2):
        grams[ids[2 + place]] = own_grams[place]
    for place in range(4):
        grams[ids[4 + place]] = near_grams[place]
    gram = grams[0]
    for place in range(1, 8):
        gram = gram + grams[place]
    flat = new * new // held
    gram = jnp.concatenate([gram[row : row + flat] for row in range(0, new, flat)], axis=1)
    out[...] = jnp.concatenate([second, gram], axis=0) * (1.0 / total)


def second_coefficients(mode, split, mass, blocks, total, *others):
    new, unit = blocks[0].shape
    held, count = split[0].shape[0], len(blocks)
    pieces = pltpu.VMEM((count, 3 * new, unit), BF16)
    scratch = [pltpu.VMEM((2 * held, 3 * new), F32), pieces, pieces]
    if mode == "far":
        shapes = [array(new + new * new // held, held)]
        scratch.insert(0, pltpu.VMEM((8, new, new), F32))
    else:
        shapes = [array(new, held), array(count, new, new)]
    return pl.pallas_call(
        functools.partial(second_kernel, count, total, mode),
        out_shape=shapes,
        in_specs=[VMEM] * (5 + count + len(others)),
        out_specs=[VMEM] * len(shapes),
        scratch_shapes=scratch,
        compiler_params=PARAMS,
        cost_estimate=cost(14 * held * new * count * unit, 4 * (held + new) * count * unit),
    )(*split, mass, *blocks, *others)


def corrections_kernel(names, bases, coef, he, ho, le, lo, *refs):
    base, outs = refs[:bases], refs[bases:]
    new, unit = outs[0].shape
    half = unit // 2
    pieces = thirds(coef[:new, :])
    pieces = jnp.concatenate([pieces, pieces], axis=1)
    places = places_of(*names)
    for which, place in enumerate(places):
        taken_off = which - (len(places) - bases)
        for start in range(0, unit, STEP):
            span, here = columns(place, half, start % half, STEP), pl.ds(start, STEP)
            high, low = (he, le) if start < half else (ho, lo)
            term = dot_nn(pieces, jnp.concatenate([high[:, span], low[:, span]], axis=0))
            term = fold_rows(term, new)
            outs[which][:, here] = base[taken_off][:, here] - term if taken_off >= 0 else term


def corrections(names, coef, split, new, unit, base=()):
    held, count = split[0].shape[0], 2 * len(names)
    return pl.pallas_call(
        functools.partial(corrections_kernel, names, len(base)),
        out_shape=[array(new, unit)] * count,
        in_specs=[VMEM] * (5 + len(base)),
        out_specs=[VMEM] * count,
        compiler_params=PARAMS,
        cost_estimate=cost(12 * held * new * count * unit, 4 * (held + new) * count * unit),
    )(coef, *split, *base)


def take_off_kernel(*refs):
    for place in range(2):
        refs[6 + place][...] = refs[place][...] - refs[2 + place][...] - refs[4 + place][...]


def eliminate(gram):
    size = gram.shape[0]
    shape = (size, 2 * size)
    rows = lax.broadcasted_iota(jnp.int32, shape, 0)
    lanes = lax.broadcasted_iota(jnp.int32, shape, 1)
    eye = (rows[:, :size] == lanes[:, :size]).astype(F32)
    work = jnp.concatenate([gram, eye], axis=1)
    for start in range(0, size, GROUP):
        group = range(start, start + GROUP)
        column = {k: jnp.broadcast_to(work[:, k : k + 1], shape) for k in group}
        line = {k: work[k : k + 1, :] for k in group}
        for k in group:
            inverse = 1.0 / column[k][k : k + 1, :]
            scaled = line[k] * inverse
            for later in range(k + 1, start + GROUP):
                line[later] = line[later] - column[k][later : later + 1, :] * scaled
                column[later] = column[later] - column[k] * (column[later][k : k + 1, :] * inverse)
            work = work - jnp.where(rows > k, column[k], 0.0) * scaled
    pivots = jnp.sum(jnp.where(lanes == rows, work, 0.0), axis=1, keepdims=True)
    scale = lax.rsqrt(pivots)
    work = work * (scale * (1.5 - 0.5 * pivots * scale * scale))
    upper = jnp.where(lanes >= rows, work, 0.0)[:, :size]
    return upper, work[:, size:]


def spread(matrix):
    pieces = thirds(matrix)
    return jnp.concatenate([pieces, pieces, pieces], axis=1)


def apply_left(spread_matrix, block):
    return fold_rows(dot_nn(spread_matrix, thirds(block)), block.shape[0])


def gram_of(block, mass):
    size = block.shape[0]
    return fold_gram(dot_nt(thirds(block * mass), thirds(block)), size)


def factor_kernel(both, upper_out, inverse_out):
    size = upper_out.shape[0]
    packed = both[size:, :]
    gram = jnp.concatenate([packed[:, lane : lane + size] for lane in range(0, packed.shape[1], size)], axis=0)
    upper_out[...], inverse_out[...] = eliminate(gram)


def middle_kernel(total, mass, inverse, *refs):
    ins, outs = refs[:6], refs[6:]
    new, unit = ins[0].shape
    left = spread(inverse[...])
    places = places_of("own")
    acc = jnp.zeros((new, new), F32)
    for which, place in enumerate(places):
        for start in range(0, unit, STEP):
            span = pl.ds(start, STEP)
            projected = ins[which][:, span] - ins[2 + which][:, span] - ins[4 + which][:, span]
            middle = apply_left(left, projected)
            outs[0][pl.ds(which * new, new), span] = middle
            acc = acc + gram_of(middle, mass[:, columns(place, unit, start, STEP)])
    outs[1][...] = acc * (1.0 / total)


def last_kernel(gram, one, two, three, upper_one, factor_out, inverse_out):
    upper, inverse = eliminate((gram[...] + one[...]) + (two[...] + three[...]))
    factor_out[...] = jnp.dot(
        upper, upper_one[...], precision=lax.Precision.HIGHEST, preferred_element_type=F32
    )
    inverse_out[...] = inverse


def finish_kernel(order, given, inverse, *refs):
    blocks, (out, buf, sems) = refs[:given], refs[-3:]
    new, unit = buf.shape[1:]
    left = spread(inverse[...])
    stack = blocks[0].shape[0] // new
    copies = []
    for which, place in enumerate(places_of(*order)):
        rows = pl.ds(which % stack * new, new)
        for start in range(0, unit, STEP):
            span = pl.ds(start, STEP)
            buf[which, :, span] = apply_left(left, blocks[which // stack][rows, span])
        copy = pltpu.make_async_copy(buf.at[which], out.at[:, columns(place, unit)], sems.at[which])
        copy.start()
        copies.append(copy)
    for copy in copies:
        copy.wait()


def finish(order, inverse, blocks, new, rows, target=None):
    unit = blocks[0].shape[1]
    given, count = len(blocks), len(blocks) * blocks[0].shape[0] // new
    extra = [] if target is None else [target]
    return pl.pallas_call(
        functools.partial(finish_kernel, order, given),
        out_shape=array(new, rows),
        in_specs=[VMEM] * (1 + given) + [HBM] * len(extra),
        out_specs=HBM,
        scratch_shapes=[pltpu.VMEM((count, new, unit), F32), pltpu.SemaphoreType.DMA((count,))],
        input_output_aliases={} if target is None else {1 + given: 0},
        compiler_params=PARAMS,
        cost_estimate=cost(18 * new * new * count * unit, 8 * new * count * unit),
    )(inverse, *blocks, *extra)


def flip(x, axis, bit):
    size = lax.axis_size(axis)
    return lax.ppermute(x, axis, [(i, i ^ bit) for i in range(size)])


def sum_over(x, axis):
    size = lax.axis_size(axis)
    bit = 1
    while bit < size:
        x = x + flip(x, axis, bit)
        bit *= 2
    return x


def local(locked, vectors, mass):
    new, rows = vectors.shape
    total = rows * lax.axis_size("row")
    unit = rows // 8
    first, *split, mass, here_a, here_b = first_coefficients(locked, vectors, mass.reshape(1, rows), unit, total)

    def scatter_sum(coef, base):
        a1, b1 = corrections(("away_first",), coef, split, new, unit)
        ra1, rb1 = flip(a1, "col", 1), flip(b1, "col", 2)
        a2, b2 = corrections(("away_second",), coef, split, new, unit)
        ra2, rb2 = flip(a2, "col", 1), flip(b2, "col", 2)
        a3, b3, a4, b4 = corrections(("pass_on", "own"), coef, split, new, unit, base)
        ra3, rb3 = flip(a3 + ra1, "col", 2), flip(b3 + rb1, "col", 1)
        return a4, b4, ra2, rb2, ra3, rb3

    first = sum_over(first, "row")
    once = pl.pallas_call(
        take_off_kernel,
        out_shape=[array(new, unit)] * 2,
        in_specs=[VMEM] * 6,
        out_specs=[VMEM] * 2,
        compiler_params=PARAMS,
        cost_estimate=cost(6 * new * unit, 32 * new * unit),
    )(*scatter_sum(first, (here_a, here_b)))
    a, b = once
    ay, bx = flip(a, "col", 2), flip(b, "col", 1)
    ax, by = flip(a, "col", 1), flip(b, "col", 2)
    far = flip(ay, "col", 1), flip(bx, "col", 2)
    second, grams = second_coefficients("own", split, mass, once, total)
    second, more = second_coefficients("near", split, mass, (ay, bx, ax, by), total, second)
    (second,) = second_coefficients("far", split, mass, far, total, second, grams, more)
    second = sum_over(second, "row")
    parts = scatter_sum(second, once)

    upper, inverse = pl.pallas_call(
        factor_kernel,
        out_shape=[array(new, new)] * 2,
        in_specs=[VMEM],
        out_specs=[VMEM] * 2,
        compiler_params=PARAMS,
        cost_estimate=cost(1e6, 1e5),
    )(second)
    pair, gram = pl.pallas_call(
        functools.partial(middle_kernel, total),
        out_shape=[array(2 * new, unit), array(new, new)],
        in_specs=[VMEM] * 8,
        out_specs=[VMEM] * 2,
        compiler_params=PARAMS,
        cost_estimate=cost(36 * new * new * 2 * unit, 24 * new * unit),
    )(mass, inverse, *parts)
    over_x, over_y = flip(pair, "col", 1), flip(pair, "col", 2)
    gram = sum_over(gram, "row")
    one, two, three = (flip(gram, "col", n) for n in (1, 2, 3))
    far = flip(over_y[:new], "col", 1), flip(over_x[new:], "col", 2)
    factor, inverse = pl.pallas_call(
        last_kernel,
        out_shape=[array(new, new)] * 2,
        in_specs=[VMEM] * 5,
        out_specs=[VMEM] * 2,
        compiler_params=PARAMS,
        cost_estimate=cost(5e9, 1e5),
    )(gram, one, two, three, upper)
    appended = finish(("own", "over_x", "over_y"), inverse, (pair, over_x, over_y), new, rows)
    appended = finish(FAR, inverse, far, new, rows, appended)
    return (appended, factor)


def solution(mesh):
    return jax.shard_map(
        local,
        mesh=mesh,
        in_specs=(P("col", "row"), P(None, "row"), P("row")),
        out_specs=(P(None, "row"), P()),
        check_vma=False,
    )
```

```python
import functools

import jax
import jax.numpy as jnp
from jax import lax
from jax.experimental import pallas as pl
from jax.experimental.pallas import tpu as pltpu
from jax.sharding import PartitionSpec as P

F32 = jnp.float32
BF16 = jnp.bfloat16
STEP = 1024
SLOTS = 4
ROWS = 16
GROUP = 4
VMEM_LIMIT = 24 * 1024 * 1024
VMEM = pl.BlockSpec(memory_space=pltpu.VMEM)
HBM = pl.BlockSpec(memory_space=pltpu.HBM)
NEAR, FAR = ("pass_on", "away_second"), ("away_first",)
PARAMS = pltpu.CompilerParams(vmem_limit_bytes=VMEM_LIMIT)


def halves(x):
    scaled = x * 65537.0
    high = scaled - (scaled - x)
    return high.astype(BF16), (x - high).astype(BF16)


def thirds(x):
    high = x.astype(BF16)
    rest = x - high.astype(F32)
    middle = rest.astype(BF16)
    low = (rest - middle.astype(F32)).astype(BF16)
    return jnp.concatenate([high, middle, low], axis=0)


def put_halves(high, low, span, source):
    for row in range(0, source.shape[0], ROWS):
        here = pl.ds(row, ROWS)
        high[here, span], low[here, span] = halves(source[here, :])


def put_pieces(target, source, weights=None):
    size = source.shape[0]
    count = target.shape[0] // size
    for row in range(0, size, ROWS):
        rest = source[pl.ds(row, ROWS), :]
        rest = rest if weights is None else rest * weights
        for piece in range(count):
            part = rest.astype(BF16)
            target[pl.ds(piece * size + row, ROWS), :] = part
            if piece + 1 < count:
                rest = rest - part.astype(F32)


def dot_nt(a, b):
    return lax.dot_general(a, b, (((1,), (1,)), ((), ())), preferred_element_type=F32)


def dot_nn(a, b):
    return lax.dot_general(a, b, (((1,), (0,)), ((), ())), preferred_element_type=F32)


def fold_rows(x, size):
    return (x[2 * size :] + x[size : 2 * size]) + x[:size]


def cost(flops, nbytes):
    return pl.CostEstimate(flops=int(flops), bytes_accessed=int(nbytes), transcendentals=0)


def array(*shape, dtype=F32):
    return jax.ShapeDtypeStruct(shape, dtype)


def columns(place, unit, start=0, width=None):
    return pl.ds(pl.multiple_of(place * unit + start, STEP), unit if width is None else width)


def unit_places():
    col = lax.axis_index("col")
    i, j = lax.rem(col, 2), lax.div(col, 2)
    k, m = 1 - i, 1 - j
    return {
        "own": (2 * i + j, 4 + 2 * j + i),
        "pass_on": (2 * i + m, 4 + 2 * j + k),
        "away_first": (2 * k + m, 4 + 2 * m + k),
        "away_second": (2 * k + j, 4 + 2 * m + i),
        "over_x": (2 * k + j, 4 + 2 * j + k),
        "over_y": (2 * i + m, 4 + 2 * m + i),
    }


def places_of(*names):
    places = unit_places()
    return [place for name in names for place in places[name]]


def first_kernel(
    total, locked, vectors, mass, out, he, ho, le, lo, mass_out, here_a, here_b, held_buf, new_buf, pe, po, acc, sems, more_sems
):
    held, rows = locked.shape
    unit = here_a.shape[1]
    chunk = unit // 2
    count = rows // chunk
    high, low, pieces = (he, ho), (le, lo), (pe, po)

    def copies(index):
        span, slot = pl.ds(index * chunk, chunk), index % SLOTS
        return (
            pltpu.make_async_copy(vectors.at[:, span], new_buf.at[slot], sems.at[0, slot]),
            pltpu.make_async_copy(locked.at[:, span], held_buf.at[slot], sems.at[1, slot]),
        )

    mass_copy = pltpu.make_async_copy(mass, mass_out, more_sems.at[0])
    mass_copy.start()
    for index in range(min(SLOTS - 1, count)):
        for copy in copies(index):
            copy.start()
    places = places_of("own")
    own_copies = [
        pltpu.make_async_copy(vectors.at[:, columns(place, unit)], here, more_sems.at[1 + which])
        for which, (place, here) in enumerate(zip(places, (here_a, here_b)))
    ]
    mass_copy.wait()
    for index in range(count + 1):
        if index < count:
            if index + SLOTS - 1 < count:
                for copy in copies(index + SLOTS - 1):
                    copy.start()
            if index == count // 2:
                for copy in own_copies:
                    copy.start()
            for copy in copies(index):
                copy.wait()
        if index < count:
            half, slot = index % 2, index % SLOTS
            put_pieces(pieces[half], new_buf.at[slot], mass_out[:, pl.ds(index * chunk, chunk)])
            put_halves(high[half], low[half], pl.ds(index // 2 * chunk, chunk), held_buf.at[slot])
        if index > 0:
            half, span = (index - 1) % 2, pl.ds((index - 1) // 2 * chunk, chunk)
            left = jnp.concatenate([high[half][:, span], low[half][:, span]], axis=0)
            term = dot_nt(left, pieces[half][...])
            if index == 1:
                acc[...] = term
            else:
                acc[...] += term
    for copy in own_copies:
        copy.wait()
    both = (acc[held:] + acc[:held]).T
    new = out.shape[0]
    out[...] = (both[new:] + both[:new]) * (1.0 / total)


def first_coefficients(locked, vectors, mass, unit, total):
    (held, rows), new = locked.shape, vectors.shape[0]
    chunk = unit // 2
    slots = min(SLOTS, rows // chunk)
    in_hbm = [pltpu.with_memory_space_constraint(x, pltpu.HBM) for x in (locked, vectors, mass)]
    return pl.pallas_call(
        functools.partial(first_kernel, total),
        out_shape=[
            array(new, held),
            *[array(held, rows // 2, dtype=BF16)] * 4,
            array(1, rows),
            array(new, unit),
            array(new, unit),
        ],
        in_specs=[HBM] * 3,
        out_specs=[VMEM] * 8,
        scratch_shapes=[
            pltpu.VMEM((slots, held, chunk), F32),
            pltpu.VMEM((slots, new, chunk), F32),
            pltpu.VMEM((2 * new, chunk), BF16),
            pltpu.VMEM((2 * new, chunk), BF16),
            pltpu.VMEM((2 * held, 2 * new), F32),
            pltpu.SemaphoreType.DMA((2, slots)),
            pltpu.SemaphoreType.DMA((3,)),
        ],
        compiler_params=PARAMS,
        cost_estimate=cost(12 * held * new * rows, 8 * held * rows),
    )(*in_hbm)


def fold_gram(x, size):
    part = fold_rows(x, size)
    return (part[:, 2 * size :] + part[:, size : 2 * size]) + part[:, :size]


def second_kernel(count, total, mode, he, ho, le, lo, mass, *refs):
    blocks, rest = refs[:count], refs[count:]
    new, unit = blocks[0].shape
    held = he.shape[0]
    rest, (acc, plain, weighted) = rest[:-3], rest[-3:]
    if mode == "own":
        out, grams = rest
    elif mode == "near":
        base, out, grams = rest
    else:
        base, own_grams, near_grams, out, grams = rest
    parts = {"own": ("own",), "near": NEAR, "far": FAR + ("own",) + NEAR}[mode]
    ids = places_of(*parts)
    for place in range(count):
        put_pieces(weighted.at[place], blocks[place], mass[:, columns(ids[place], unit)])
        put_pieces(plain.at[place], blocks[place])
        span = columns(ids[place], unit // 2)
        high = jnp.concatenate([he[:, span], ho[:, span]], axis=1)
        low = jnp.concatenate([le[:, span], lo[:, span]], axis=1)
        left = jnp.concatenate([high, low, plain[place]], axis=0)
        term = dot_nt(left, weighted[place])
        grams[ids[place] if mode == "far" else place] = fold_gram(term[2 * held :], new)
        if place == 0:
            acc[...] = term[: 2 * held]
        else:
            acc[...] += term[: 2 * held]
    second = fold_rows((acc[:held] + acc[held:]).T, new)
    if mode != "own":
        second = second + base[...]
    if mode != "far":
        out[...] = second
        return
    for place in range(2):
        grams[ids[2 + place]] = own_grams[place]
    for place in range(4):
        grams[ids[4 + place]] = near_grams[place]
    gram = grams[0]
    for place in range(1, 8):
        gram = gram + grams[place]
    flat = new * new // held
    gram = jnp.concatenate([gram[row : row + flat] for row in range(0, new, flat)], axis=1)
    out[...] = jnp.concatenate([second, gram], axis=0) * (1.0 / total)


def second_coefficients(mode, split, mass, blocks, total, *others):
    new, unit = blocks[0].shape
    held, count = split[0].shape[0], len(blocks)
    pieces = pltpu.VMEM((count, 3 * new, unit), BF16)
    scratch = [pltpu.VMEM((2 * held, 3 * new), F32), pieces, pieces]
    if mode == "far":
        shapes = [array(new + new * new // held, held)]
        scratch.insert(0, pltpu.VMEM((8, new, new), F32))
    else:
        shapes = [array(new, held), array(count, new, new)]
    return pl.pallas_call(
        functools.partial(second_kernel, count, total, mode),
        out_shape=shapes,
        in_specs=[VMEM] * (5 + count + len(others)),
        out_specs=[VMEM] * len(shapes),
        scratch_shapes=scratch,
        compiler_params=PARAMS,
        cost_estimate=cost(14 * held * new * count * unit, 4 * (held + new) * count * unit),
    )(*split, mass, *blocks, *others)


def corrections_kernel(names, bases, coef, he, ho, le, lo, *refs):
    base, outs = refs[:bases], refs[bases:]
    new, unit = outs[0].shape
    half = unit // 2
    pieces = thirds(coef[:new, :])
    pieces = jnp.concatenate([pieces, pieces], axis=1)
    places = places_of(*names)
    for which, place in enumerate(places):
        taken_off = which - (len(places) - bases)
        for start in range(0, unit, STEP):
            span, here = columns(place, half, start % half, STEP), pl.ds(start, STEP)
            high, low = (he, le) if start < half else (ho, lo)
            term = dot_nn(pieces, jnp.concatenate([high[:, span], low[:, span]], axis=0))
            term = fold_rows(term, new)
            outs[which][:, here] = base[taken_off][:, here] - term if taken_off >= 0 else term


def corrections(names, coef, split, new, unit, base=()):
    held, count = split[0].shape[0], 2 * len(names)
    return pl.pallas_call(
        functools.partial(corrections_kernel, names, len(base)),
        out_shape=[array(new, unit)] * count,
        in_specs=[VMEM] * (5 + len(base)),
        out_specs=[VMEM] * count,
        compiler_params=PARAMS,
        cost_estimate=cost(12 * held * new * count * unit, 4 * (held + new) * count * unit),
    )(coef, *split, *base)


def take_off_kernel(*refs):
    for place in range(2):
        refs[6 + place][...] = refs[place][...] - refs[2 + place][...] - refs[4 + place][...]


def eliminate(gram):
    size = gram.shape[0]
    shape = (size, 2 * size)
    rows = lax.broadcasted_iota(jnp.int32, shape, 0)
    lanes = lax.broadcasted_iota(jnp.int32, shape, 1)
    eye = (rows[:, :size] == lanes[:, :size]).astype(F32)
    work = jnp.concatenate([gram, eye], axis=1)
    for start in range(0, size, GROUP):
        group = range(start, start + GROUP)
        column = {k: jnp.broadcast_to(work[:, k : k + 1], shape) for k in group}
        line = {k: work[k : k + 1, :] for k in group}
        for k in group:
            inverse = 1.0 / column[k][k : k + 1, :]
            scaled = line[k] * inverse
            for later in range(k + 1, start + GROUP):
                line[later] = line[later] - column[k][later : later + 1, :] * scaled
                column[later] = column[later] - column[k] * (column[later][k : k + 1, :] * inverse)
            work = work - jnp.where(rows > k, column[k], 0.0) * scaled
    pivots = jnp.sum(jnp.where(lanes == rows, work, 0.0), axis=1, keepdims=True)
    scale = lax.rsqrt(pivots)
    work = work * (scale * (1.5 - 0.5 * pivots * scale * scale))
    upper = jnp.where(lanes >= rows, work, 0.0)[:, :size]
    return upper, work[:, size:]


def spread(matrix):
    pieces = thirds(matrix)
    return jnp.concatenate([pieces, pieces, pieces], axis=1)


def apply_left(spread_matrix, block):
    return fold_rows(dot_nn(spread_matrix, thirds(block)), block.shape[0])


def gram_of(block, mass):
    size = block.shape[0]
    return fold_gram(dot_nt(thirds(block * mass), thirds(block)), size)


def factor_kernel(both, upper_out, inverse_out):
    size = upper_out.shape[0]
    packed = both[size:, :]
    gram = jnp.concatenate([packed[:, lane : lane + size] for lane in range(0, packed.shape[1], size)], axis=0)
    upper_out[...], inverse_out[...] = eliminate(gram)


def middle_kernel(total, mass, inverse, *refs):
    ins, outs = refs[:6], refs[6:]
    new, unit = ins[0].shape
    left = spread(inverse[...])
    places = places_of("own")
    acc = jnp.zeros((new, new), F32)
    for which, place in enumerate(places):
        for start in range(0, unit, STEP):
            span = pl.ds(start, STEP)
            projected = ins[which][:, span] - ins[2 + which][:, span] - ins[4 + which][:, span]
            middle = apply_left(left, projected)
            outs[0][pl.ds(which * new, new), span] = middle
            acc = acc + gram_of(middle, mass[:, columns(place, unit, start, STEP)])
    outs[1][...] = acc * (1.0 / total)


def last_kernel(gram, one, two, three, upper_one, factor_out, inverse_out):
    upper, inverse = eliminate((gram[...] + one[...]) + (two[...] + three[...]))
    factor_out[...] = jnp.dot(
        upper, upper_one[...], precision=lax.Precision.HIGHEST, preferred_element_type=F32
    )
    inverse_out[...] = inverse


def finish_kernel(order, given, inverse, *refs):
    blocks, (out, buf, sems) = refs[:given], refs[-3:]
    new, unit = buf.shape[1:]
    left = spread(inverse[...])
    stack = blocks[0].shape[0] // new
    copies = []
    for which, place in enumerate(places_of(*order)):
        rows = pl.ds(which % stack * new, new)
        for start in range(0, unit, STEP):
            span = pl.ds(start, STEP)
            buf[which, :, span] = apply_left(left, blocks[which // stack][rows, span])
        copy = pltpu.make_async_copy(buf.at[which], out.at[:, columns(place, unit)], sems.at[which])
        copy.start()
        copies.append(copy)
    for copy in copies:
        copy.wait()


def finish(order, inverse, blocks, new, rows, target=None):
    unit = blocks[0].shape[1]
    given, count = len(blocks), len(blocks) * blocks[0].shape[0] // new
    extra = [] if target is None else [target]
    return pl.pallas_call(
        functools.partial(finish_kernel, order, given),
        out_shape=array(new, rows),
        in_specs=[VMEM] * (1 + given) + [HBM] * len(extra),
        out_specs=HBM,
        scratch_shapes=[pltpu.VMEM((count, new, unit), F32), pltpu.SemaphoreType.DMA((count,))],
        input_output_aliases={} if target is None else {1 + given: 0},
        compiler_params=PARAMS,
        cost_estimate=cost(18 * new * new * count * unit, 8 * new * count * unit),
    )(inverse, *blocks, *extra)


def flip(x, axis, bit):
    size = lax.axis_size(axis)
    return lax.ppermute(x, axis, [(i, i ^ bit) for i in range(size)])


def sum_over(x, axis):
    size = lax.axis_size(axis)
    bit = 1
    while bit < size:
        x = x + flip(x, axis, bit)
        bit *= 2
    return x


def local(locked, vectors, mass):
    new, rows = vectors.shape
    total = rows * lax.axis_size("row")
    unit = rows // 8
    first, *split, mass, here_a, here_b = first_coefficients(locked, vectors, mass.reshape(1, rows), unit, total)

    def scatter_sum(coef, base):
        a1, b1 = corrections(("away_first",), coef, split, new, unit)
        ra1, rb1 = flip(a1, "col", 1), flip(b1, "col", 2)
        a2, b2 = corrections(("away_second",), coef, split, new, unit)
        ra2, rb2 = flip(a2, "col", 1), flip(b2, "col", 2)
        a3, b3, a4, b4 = corrections(("pass_on", "own"), coef, split, new, unit, base)
        ra3, rb3 = flip(a3 + ra1, "col", 2), flip(b3 + rb1, "col", 1)
        return a4, b4, ra2, rb2, ra3, rb3

    first = sum_over(first, "row")
    once = pl.pallas_call(
        take_off_kernel,
        out_shape=[array(new, unit)] * 2,
        in_specs=[VMEM] * 6,
        out_specs=[VMEM] * 2,
        compiler_params=PARAMS,
        cost_estimate=cost(6 * new * unit, 32 * new * unit),
    )(*scatter_sum(first, (here_a, here_b)))
    a, b = once
    ay, bx = flip(a, "col", 2), flip(b, "col", 1)
    ax, by = flip(a, "col", 1), flip(b, "col", 2)
    far = flip(ay, "col", 1), flip(bx, "col", 2)
    second, grams = second_coefficients("own", split, mass, once, total)
    second, more = second_coefficients("near", split, mass, (ay, bx, ax, by), total, second)
    (second,) = second_coefficients("far", split, mass, far, total, second, grams, more)
    second = sum_over(second, "row")
    parts = scatter_sum(second, once)

    upper, inverse = pl.pallas_call(
        factor_kernel,
        out_shape=[array(new, new)] * 2,
        in_specs=[VMEM],
        out_specs=[VMEM] * 2,
        compiler_params=PARAMS,
        cost_estimate=cost(1e6, 1e5),
    )(second)
    pair, gram = pl.pallas_call(
        functools.partial(middle_kernel, total),
        out_shape=[array(2 * new, unit), array(new, new)],
        in_specs=[VMEM] * 8,
        out_specs=[VMEM] * 2,
        compiler_params=PARAMS,
        cost_estimate=cost(36 * new * new * 2 * unit, 24 * new * unit),
    )(mass, inverse, *parts)
    over_x, over_y = flip(pair, "col", 1), flip(pair, "col", 2)
    gram = sum_over(gram, "row")
    one, two, three = (flip(gram, "col", n) for n in (1, 2, 3))
    far = flip(over_y[:new], "col", 1), flip(over_x[new:], "col", 2)
    factor, inverse = pl.pallas_call(
        last_kernel,
        out_shape=[array(new, new)] * 2,
        in_specs=[VMEM] * 5,
        out_specs=[VMEM] * 2,
        compiler_params=PARAMS,
        cost_estimate=cost(5e9, 1e5),
    )(gram, one, two, three, upper)
    appended = finish(("own", "over_x", "over_y"), inverse, (pair, over_x, over_y), new, rows)
    appended = finish(FAR, inverse, far, new, rows, appended)
    return (appended, factor)


def solution(mesh):
    return jax.shard_map(
        local,
        mesh=mesh,
        in_specs=(P("col", "row"), P(None, "row"), P("row")),
        out_specs=(P(None, "row"), P()),
        check_vma=False,
    )
```
